128 devices in a mesh: ctx: 4 (over x), head: 32 (over z, y, core).
Axes of the slice: x: 4, y: 4, z: 4, core: 2. Of those that a mesh axis runs over, the one named last changes fastest.
Arguments:
- prefix_x: bfloat16 [4, 1536, 16384], P(None, 'ctx', 'head'), may hold values from -6 to 6
- prefix_bc: bfloat16 [4, 1536, 2048], P(None, 'ctx', 'head'), may hold values from -6 to 6
- prefix_gate: bfloat16 [4, 1536, 16384], P(None, 'ctx', 'head'), may hold values from -6 to 6
- prefix_steps: float32 [4, 1536, 256], P(None, 'ctx', 'head'), may hold values from -4 to 4
- x_kernel: bfloat16 [4, 16384], P(None, 'head'), may hold values from -3 to 3
- bc_kernel: bfloat16 [4, 2048], P(None, 'head'), may hold values from -3 to 3
- step_bias: float32 [256], P('head'), may hold values from -3 to -1
- log_rate: float32 [256], P('head'), may hold values from -6.2 to -1.4
- skip_gain: float32 [256], P('head'), may hold values from 0.5 to 1.5
- norm_gain: float32 [16384], replicated, may hold values from 0.5 to 1.5
- option_x: bfloat16 [16, 256, 16384], P('ctx', None, 'head'), may hold values from -6 to 6
- option_bc: bfloat16 [16, 256, 2048], P('ctx', None, 'head'), may hold values from -6 to 6
- option_gate: bfloat16 [16, 256, 16384], P('ctx', None, 'head'), may hold values from -6 to 6
- option_steps: float32 [16, 256, 256], P('ctx', None, 'head'), may hold values from -4 to 4
- option_len: int32 [16], P('ctx'), may hold values from 64 to 256, as said below
Outputs:
- prefix_out: bfloat16 [4, 1536, 16384], P(None, ('ctx', 'head'))
- option_out: bfloat16 [16, 256, 16384], P('ctx', 'head')
The draws below stay inside these ranges and needn't reach their ends.
Inputs may be any that keep to these rules, and one draw needn't show every extreme that they name: `option_len`: some option has the full length 256 in every draw.
All inputs are finite; a program needn't handle non-finite values.
Results may differ from the reference program's by a relative error of at most 0.0051.
Values may be sent and summed in bfloat16 or wider, within the bound.
A program may use at most 128 MiB of HBM per device.

```python
import math
import jax
import jax.numpy as jnp
from jax import lax

HEADS = 256
HEAD_DIM = 64
NS = 128
GROUPS = 8
CONV = 4
INNER = 16384
SEQS = 4
OPTS = 4
OLEN = 256
LPRE = 1536
NOPT = 16


def draw_option_len(key, part):
    key = jax.random.fold_in(key, 5)
    first_key, second_key = jax.random.split(key)
    lengths = jax.random.randint(first_key, (NOPT,), OLEN // 4, OLEN + 1)
    chosen = jax.random.randint(second_key, (), 0, NOPT)
    return jnp.where(jnp.arange(NOPT) == chosen, OLEN, lengths).astype(jnp.int32)


def levels(rng, shape, shards, smallest, top_value):
    level = 1.0
    for position, parts in shards:
        draws = jax.random.uniform(jax.random.fold_in(jax.random.fold_in(rng, 6), position), (parts,), jnp.float32, smallest / len(shards), top_value / len(shards))
        level = level * jnp.repeat(jnp.exp(draws), shape[position] // parts).reshape((-1,) + (1,) * (len(shape) - 1 - position))
    return level


def noise(own_key, dims, scale, bound, cuts=(), held_as=jnp.bfloat16):
    values = jax.random.normal(own_key, dims, jnp.float32) * scale
    if len(cuts) > 0:
        values = levels(own_key, dims, cuts, -0.22, 0.18) * values
    return jnp.clip(values, min=-bound, max=bound).astype(held_as)


def setup_inputs(seed: int = 0) -> dict:
    streams_of = jax.random.split(jax.random.key(seed), 16)
    prefix_x = noise(streams_of[0], (SEQS, LPRE, INNER), 1.0, 6.0, ((1, 4), (2, 32)))
    prefix_bc = noise(streams_of[1], (SEQS, LPRE, 2 * GROUPS * NS), 1.0, 6.0, ((1, 4), (2, 32)))
    prefix_gate = noise(streams_of[2], (SEQS, LPRE, INNER), 1.0, 6.0, ((1, 4), (2, 32)))
    prefix_steps = noise(streams_of[3], (SEQS, LPRE, HEADS), 1.0, 4.0, ((1, 4), (2, 32)), jnp.float32)
    x_kernel = noise(streams_of[4], (CONV, INNER), CONV ** -0.5, 3.0, ((1, 32),))
    bc_kernel = noise(streams_of[5], (CONV, 2 * GROUPS * NS), CONV ** -0.5, 3.0, ((1, 32),))
    step_bias = jnp.clip(-3.0 + 2.0 * jax.random.uniform(streams_of[6], (HEADS,), jnp.float32) ** levels(streams_of[6], (HEADS,), ((0, 32),), -0.2, 0.2), -3.0, -1.0)
    log_rate = jnp.clip(-6.2 + 4.7999998 * jax.random.uniform(streams_of[7], (HEADS,), jnp.float32) ** levels(streams_of[7], (HEADS,), ((0, 32),), -0.2, 0.2), -6.2, -1.4)
    skip_gain = jnp.clip(0.5 + 1.0 * jax.random.uniform(streams_of[8], (HEADS,), jnp.float32) ** levels(streams_of[8], (HEADS,), ((0, 32),), -0.2, 0.2), 0.5, 1.5)
    norm_gain = jnp.clip(1.0 + 0.1 * jax.random.normal(streams_of[9], (INNER,), jnp.float32), 0.5, 1.5)
    option_x = noise(streams_of[10], (NOPT, OLEN, INNER), 1.0, 6.0, ((0, 4), (2, 32)))
    option_bc = noise(streams_of[11], (NOPT, OLEN, 2 * GROUPS * NS), 1.0, 6.0, ((0, 4), (2, 32)))
    option_gate = noise(streams_of[12], (NOPT, OLEN, INNER), 1.0, 6.0, ((0, 4), (2, 32)))
    option_steps = noise(streams_of[13], (NOPT, OLEN, HEADS), 1.0, 4.0, ((0, 4), (2, 32)), jnp.float32)
    option_len = draw_option_len(jax.random.fold_in(streams_of[15], 71), 0)
    return dict(prefix_x=prefix_x, prefix_bc=prefix_bc, prefix_gate=prefix_gate, prefix_steps=prefix_steps, x_kernel=x_kernel, bc_kernel=bc_kernel, step_bias=step_bias, log_rate=log_rate, skip_gain=skip_gain, norm_gain=norm_gain, option_x=option_x, option_bc=option_bc, option_gate=option_gate, option_steps=option_steps, option_len=option_len)


epsilon = 1e-05
highest = lax.Precision.HIGHEST

def causal_conv(sequence, kernel, context):
    length = sequence.shape[1]
    joined = jnp.concatenate([context, sequence], axis=1).astype(jnp.float32)
    weights = kernel.astype(jnp.float32)
    summed = joined[:, 0:length] * weights[0]
    for offset in range(1, weights.shape[0]):
        summed = summed + joined[:, offset:offset + length] * weights[offset]
    return jax.nn.silu(summed).astype(jnp.bfloat16)

def scan_block(carry_state, pieces, decay_rate, skip_shape):
    values = pieces[0].astype(jnp.float32)
    b_rows = pieces[1].astype(jnp.float32)
    c_rows = pieces[2].astype(jnp.float32)
    step_size = pieces[3]
    cumul = jnp.cumsum(step_size * decay_rate, axis=1)
    extent = cumul.shape[1]
    lower = lax.broadcasted_iota(jnp.int32, (extent, extent), 0) >= lax.broadcasted_iota(jnp.int32, (extent, extent), 1)
    ordered = jnp.moveaxis(cumul, 1, -1)
    spans = ordered[..., :, None] - ordered[..., None, :]
    decays = jnp.exp(jnp.where(lower, spans, -jnp.inf))
    scores = jnp.einsum('btgn,bsgn->bgts', c_rows, b_rows, precision=highest)
    weights = decays * scores[:, :, None] * jnp.moveaxis(step_size, 1, -1)[..., None, :]
    within = jnp.einsum('bgjts,bsgjp->btgjp', weights, values, precision=highest)
    carried = jnp.einsum('btgn,bgjpn->btgjp', c_rows, carry_state, precision=highest) * jnp.exp(cumul)[..., None]
    outputs = within + carried + skip_shape[:, :, None] * values
    remain = jnp.exp(cumul[:, -1:] - cumul) * step_size
    fresh = jnp.einsum('bsgjp,bsgn->bgjpn', values * remain[..., None], b_rows, precision=highest)
    new_state = jnp.exp(cumul[:, -1])[..., None, None] * carry_state + fresh
    return (new_state, outputs.astype(jnp.bfloat16))

def run_sequence(start_state, pieces, decay_rate, skip_shape, block_rows):
    batch = pieces[0].shape[0]
    length = pieces[0].shape[1]
    count = length // block_rows

    def cut(array):
        shaped = array.reshape((batch, count, block_rows) + array.shape[2:])
        return jnp.moveaxis(shaped, 1, 0)

    def advance(state_now, piece):
        return scan_block(state_now, piece, decay_rate, skip_shape)
    final_state, outputs = lax.scan(advance, start_state, tuple((cut(array) for array in pieces)))
    outputs = jnp.moveaxis(outputs, 0, 1)
    return (final_state, outputs.reshape((batch, length) + outputs.shape[3:]))

def gated_norm(values, gates, gain):
    mixed = values.astype(jnp.float32) * jax.nn.silu(gates.astype(jnp.float32))
    grouped = mixed.reshape(mixed.shape[:-1] + (GROUPS, INNER // GROUPS))
    scale = lax.rsqrt(lax.optimization_barrier(jnp.mean(grouped * grouped, axis=-1, keepdims=True)) + epsilon)
    return (grouped * scale).reshape(mixed.shape) * gain

def reference(prefix_x, prefix_bc, prefix_gate, prefix_steps, x_kernel, bc_kernel, step_bias, log_rate, skip_gain, norm_gain, option_x, option_bc, option_gate, option_steps, option_len):
    tap_count = CONV - 1
    per_group = HEADS // GROUPS
    x_conv = causal_conv(prefix_x, x_kernel, jnp.zeros((SEQS, tap_count, INNER), jnp.bfloat16))
    bc_conv = causal_conv(prefix_bc, bc_kernel, jnp.zeros((SEQS, tap_count, 2 * GROUPS * NS), jnp.bfloat16))
    owners = jnp.arange(NOPT, dtype=jnp.int32) // OPTS
    option_x_conv = causal_conv(option_x, x_kernel, prefix_x[owners, LPRE - tap_count:])
    option_bc_conv = causal_conv(option_bc, bc_kernel, prefix_bc[owners, LPRE - tap_count:])
    decay_rate = (-jnp.exp(log_rate)).reshape(GROUPS, per_group)
    skip_shape = skip_gain.reshape(GROUPS, per_group)

    def prepare(x_part, bc_part, raw_steps):
        batch = x_part.shape[0]
        length = x_part.shape[1]
        values = x_part.reshape(batch, length, GROUPS, per_group, HEAD_DIM)
        paired = bc_part.reshape(batch, length, GROUPS, 2, NS)
        step_size = jax.nn.softplus(raw_steps + step_bias).reshape(batch, length, GROUPS, per_group)
        return (values, paired[:, :, :, 0], paired[:, :, :, 1], step_size)
    start_zero = jnp.zeros((SEQS, GROUPS, per_group, HEAD_DIM, NS), jnp.float32)
    prefix_state, y_prefix = run_sequence(start_zero, prepare(x_conv, bc_conv, prefix_steps), decay_rate, skip_shape, math.gcd(LPRE, 256))
    y_prefix = y_prefix.reshape(SEQS, LPRE, INNER)
    option_start = prefix_state[owners]
    option_block = math.gcd(OLEN, 256)

    def one_option(items):
        pieces = tuple((array[None] for array in items[1:]))
        ignored, outputs = run_sequence(items[0][None], pieces, decay_rate, skip_shape, option_block)
        return outputs[0]
    y_option = lax.map(one_option, (option_start,) + prepare(option_x_conv, option_bc_conv, option_steps))
    y_option = y_option.reshape(NOPT, OLEN, INNER)

    def norm_prompt(items):
        return gated_norm(items[0], items[1], norm_gain).astype(jnp.bfloat16)
    prefix_out = lax.map(norm_prompt, (y_prefix, prefix_gate))
    keep = (lax.broadcasted_iota(jnp.int32, (NOPT, OLEN), 1) < option_len[:, None]).astype(jnp.float32)
    option_out = (gated_norm(y_option, option_gate, norm_gain) * keep[..., None]).astype(jnp.bfloat16)
    return (prefix_out, option_out)
```

```python
import functools

import jax
import jax.numpy as jnp
from jax import lax
from jax.experimental import pallas as pl
from jax.experimental.pallas import tpu as pltpu
from jax.sharding import PartitionSpec as P

NS = 128
GROUPS = 8
CHUNK = 128
HALO = 16
EPSILON = 1e-05
MESH = pl.DeviceIdType.MESH
MIB = 1 << 20


def silu(v):
    return v / (1.0 + jnp.exp(-v))


def dot(a, b, dims=((1,), (0,)), precision=None):
    return lax.dot_general(
        a, b, (dims, ((), ())), precision=precision, preferred_element_type=jnp.float32
    )


def conv_window(window, taps, rows):
    total = window[HALO - 3 : HALO - 3 + rows] * taps[0:1]
    for k in range(1, 4):
        total = total + window[HALO - 3 + k : HALO - 3 + k + rows] * taps[k : k + 1]
    return silu(total)


def mixer_kernel(
    heads,
    px, pbc, pg, pst, ox, obc, og, ost, xk, bck, sb, lr, sg,
    packed,
    xpad, xpado, gp, go, rim, gat, states, dec, xs, ee, rows, bu, cu, part, mid, ybuf, ybufo,
    load_sem, rim_send, rim_recv, bc_send, bc_recv, st_send, st_recv, dec_send, dec_recv,
):
    c = lax.axis_index("ctx")
    h = lax.axis_index("head")
    seqs, tokens, channels = px.shape
    opts, olen = ox.shape[0], ox.shape[1]
    nh = heads
    pk, ok = tokens // CHUNK, olen // CHUNK
    pchunks, chunks = seqs * pk, seqs * pk + opts * ok
    cols = pbc.shape[2]
    base = (h // 4) * 4
    r = lax.rem(h, 4)
    near = base + (r + 1 - 2 * lax.rem(r, 2))
    far = base + lax.rem(r + 2, 4)
    far_slot = lax.rem(r + 2, 4)
    half_p = seqs // 2 * tokens
    half_o = opts // 2 * olen

    loads = [
        pltpu.make_async_copy(px, xpad.at[:, pl.ds(HALO, tokens), :], load_sem.at[0]),
        pltpu.make_async_copy(ox, xpado.at[:, pl.ds(HALO, olen), :], load_sem.at[1]),
        pltpu.make_async_copy(pg, gp, load_sem.at[2]),
        pltpu.make_async_copy(og, go, load_sem.at[3]),
    ]
    for load in loads:
        load.start()

    barrier = pltpu.get_barrier_semaphore()
    for d in range(1, 4):
        pl.semaphore_signal(barrier, 1, device_id=(lax.rem(c + d, 4), h), device_id_type=MESH)
        pl.semaphore_signal(
            barrier, 1, device_id=(c, base + lax.rem(r + d, 4)), device_id_type=MESH
        )

    loads[0].wait()
    pad = jnp.zeros((HALO - 3 * seqs, channels), jnp.float32)
    tails = [xpad[s, tokens : tokens + HALO, :].astype(jnp.float32)[HALO - 3 :] for s in range(seqs)]
    rim[c, :, 0:channels] = jnp.concatenate(tails + [pad], axis=0).astype(jnp.bfloat16)
    pad = jnp.zeros((HALO - 3 * seqs, cols), jnp.float32)
    tails = [pbc[s, tokens - HALO : tokens, :].astype(jnp.float32)[HALO - 3 :] for s in range(seqs)]
    tails = jnp.concatenate(tails + [pad], axis=0)
    rim[c, :, channels : channels + 128] = jnp.concatenate(
        [tails, jnp.zeros((HALO, 128 - cols), jnp.float32)], axis=1
    ).astype(jnp.bfloat16)

    pl.semaphore_wait(barrier, 6)

    def rim_copy(d):
        return pltpu.make_async_remote_copy(
            src_ref=rim.at[c], dst_ref=rim.at[c], send_sem=rim_send.at[d - 1],
            recv_sem=rim_recv.at[d - 1], device_id=(lax.rem(c + d, 4), h), device_id_type=MESH,
        )

    def rim_arrival(d):
        source = lax.rem(c + 4 - d, 4)
        return pltpu.make_async_remote_copy(
            src_ref=rim.at[source], dst_ref=rim.at[source], send_sem=rim_send.at[d - 1],
            recv_sem=rim_recv.at[d - 1], device_id=(lax.rem(c + d, 4), h), device_id_type=MESH,
        )

    for d in range(1, 4):
        rim_copy(d).start()

    bias, rate = sb[...], -jnp.exp(lr[...])
    raw = [pst[s, k * CHUNK : (k + 1) * CHUNK, :] for s in range(seqs) for k in range(pk)]
    raw += [ost[o, k * CHUNK : (k + 1) * CHUNK, :] for o in range(opts) for k in range(ok)]
    raw = jnp.concatenate(raw, axis=1) + jnp.concatenate([bias] * chunks, axis=1)
    size = jnp.maximum(raw, 0.0) + jnp.log1p(jnp.exp(-jnp.abs(raw)))
    move = size * jnp.concatenate([rate] * chunks, axis=1)
    across = lax.broadcasted_iota(jnp.int32, (CHUNK, CHUNK), 0)
    along = lax.broadcasted_iota(jnp.int32, (CHUNK, CHUNK), 1)
    lower = across >= along
    cumul = dot(lower.astype(jnp.float32), move, precision=lax.Precision.HIGHEST)
    middle, end = cumul[CHUNK // 2 - 1 : CHUNK // 2], cumul[CHUNK - 1 : CHUNK]
    filler = jnp.zeros((13, end.shape[1]), jnp.float32)
    wide = jnp.concatenate(
        [
            jnp.exp(middle - cumul) * size,
            jnp.exp(cumul - middle),
            jnp.exp(end),
            jnp.exp(end - middle),
            jnp.exp(middle),
            filler,
        ],
        axis=0,
    )
    wide_high = wide.astype(jnp.bfloat16)
    wide_low = (wide - wide_high.astype(jnp.float32)).astype(jnp.bfloat16)
    lanes = wide.shape[1]
    per_head = channels // 8
    spread_row = lax.broadcasted_iota(jnp.int32, (lanes, channels), 0)
    spread_head = lax.div(lax.broadcasted_iota(jnp.int32, (lanes, channels), 1), per_head)

    for d in range(1, 4):
        rim_arrival(d).wait_recv()
    behind = lax.rem(c + 3, 4)
    has_behind = (c > 0).astype(jnp.float32)
    before = rim[behind].astype(jnp.float32) * has_behind
    last = rim[3].astype(jnp.float32)
    zeros = jnp.zeros((HALO - 3, channels), jnp.float32)
    owner_tail = jnp.zeros((3, channels + 128), jnp.float32)
    for s in range(seqs):
        tail = before[3 * s : 3 * s + 3]
        xpad[s, 0:HALO, :] = jnp.concatenate([zeros, tail[:, 0:channels]], axis=0).astype(jnp.bfloat16)
        owner_tail = owner_tail + last[3 * s : 3 * s + 3] * (c == s).astype(jnp.float32)
    loads[1].wait()
    for o in range(opts):
        xpado[o, 0:HALO, :] = jnp.concatenate([zeros, owner_tail[:, 0:channels]], axis=0).astype(
            jnp.bfloat16
        )

    taps = bck[...].astype(jnp.float32)
    taps = jnp.concatenate([taps, taps], axis=1)
    zeros = jnp.zeros((HALO - 3, 2 * cols), jnp.float32)
    for a in range(seqs // 2):
        tail = [before[3 * s : 3 * s + 3, channels : channels + cols] for s in (a, a + seqs // 2)]
        body = [pbc[s].astype(jnp.float32) for s in (a, a + seqs // 2)]
        window = jnp.concatenate(
            [zeros, jnp.concatenate(tail, axis=1), jnp.concatenate(body, axis=1)],
            axis=0,
        )
        gat[r, a * tokens : (a + 1) * tokens, :] = conv_window(window, taps, tokens).astype(jnp.bfloat16)
    tail = owner_tail[:, channels : channels + cols]
    tail = jnp.concatenate([tail, tail], axis=1)
    for a in range(opts // 2):
        body = [obc[o].astype(jnp.float32) for o in (a, a + opts // 2)]
        window = jnp.concatenate([zeros, tail, jnp.concatenate(body, axis=1)], axis=0)
        gat[r, half_p + a * olen : half_p + (a + 1) * olen, :] = conv_window(
            window, taps, olen
        ).astype(jnp.bfloat16)

    spans = ((0, half_p), (half_p, half_o))

    def bc_copy(part_no, way, slot, target):
        start, size_ = spans[part_no]
        ref = gat.at[slot, pl.ds(start, size_), :]
        return pltpu.make_async_remote_copy(
            src_ref=ref, dst_ref=ref, send_sem=bc_send.at[part_no, way],
            recv_sem=bc_recv.at[part_no, way], device_id=(c, target), device_id_type=MESH,
        )

    for part_no in range(2):
        bc_copy(part_no, 1, r, far).start()
        bc_copy(part_no, 0, r, near).start()

    near_slot = near - base
    cross_slot = lax.rem(near_slot + 2, 4)

    xtaps = xk[...].astype(jnp.float32)

    def convolve(j, window):
        out = conv_window(window, xtaps, CHUNK).astype(jnp.bfloat16)
        pick = (spread_row == 8 * j + spread_head).astype(jnp.bfloat16)
        grown = dot(wide_high, pick) + dot(wide_low, pick)
        xs[j] = (out.astype(jnp.float32) * grown[0:CHUNK]).astype(jnp.bfloat16)
        ee[j] = grown[CHUNK : 2 * CHUNK]
        rows[j] = grown[2 * CHUNK : 2 * CHUNK + 8]
        return out

    def prefix_conv(i, carry):
        s, k = i // pk, pk - 1 - lax.rem(i, pk)
        at = pl.multiple_of(k * CHUNK, CHUNK)
        window = xpad[s, pl.ds(at, CHUNK + HALO), :].astype(jnp.float32)
        xpad[s, pl.ds(at + HALO, CHUNK), :] = convolve(s * pk + k, window)
        return carry

    def option_conv(i, carry):
        o, k = i // ok, ok - 1 - lax.rem(i, ok)
        at = pl.multiple_of(k * CHUNK, CHUNK)
        window = xpado[o, pl.ds(at, CHUNK + HALO), :].astype(jnp.float32)
        xpado[o, pl.ds(at + HALO, CHUNK), :] = convolve(pchunks + o * ok + k, window)
        return carry

    lax.fori_loop(0, pchunks, prefix_conv, 0)
    lax.fori_loop(0, opts * ok, option_conv, 0)

    for s in range(seqs):
        total = rows[s * pk, 0:1, :]
        for k in range(1, pk):
            total = total * rows[s * pk + k, 0:1, :]
        dec[c, s : s + 1, :] = total

    def dec_copy(d, slot):
        return pltpu.make_async_remote_copy(
            src_ref=dec.at[slot], dst_ref=dec.at[slot], send_sem=dec_send.at[d - 1],
            recv_sem=dec_recv.at[d - 1], device_id=(lax.rem(c + d, 4), h), device_id_type=MESH,
        )

    for d in range(1, 4):
        dec_copy(d, c).start()

    left = lax.broadcasted_iota(jnp.int32, (CHUNK, 128), 1) < 64

    def unfold(start, low, high):
        parts = [gat[i, pl.ds(start, CHUNK), :].astype(jnp.float32) for i in range(4)]
        turned = [pltpu.roll(p, 64, 1) for p in parts]
        bu[low] = jnp.where(left, parts[0], turned[1]).astype(jnp.bfloat16)
        bu[high] = jnp.where(left, turned[0], parts[1]).astype(jnp.bfloat16)
        cu[low] = jnp.where(left, parts[2], turned[3]).astype(jnp.bfloat16)
        cu[high] = jnp.where(left, turned[2], parts[3]).astype(jnp.bfloat16)

    def unfold_prefix(i, carry):
        a, k = i // pk, lax.rem(i, pk)
        start = pl.multiple_of(i * CHUNK, CHUNK)
        unfold(start, a * pk + k, (a + seqs // 2) * pk + k)
        return carry

    def unfold_option(i, carry):
        a, k = i // ok, lax.rem(i, ok)
        start = pl.multiple_of(half_p + i * CHUNK, CHUNK)
        unfold(start, pchunks + a * ok + k, pchunks + (a + opts // 2) * ok + k)
        return carry

    bc_copy(0, 1, far_slot, far).wait_recv()
    bc_copy(0, 2, far_slot, near).start()
    bc_copy(0, 0, near_slot, near).wait_recv()
    bc_copy(0, 2, cross_slot, near).wait_recv()
    lax.fori_loop(0, seqs // 2 * pk, unfold_prefix, 0)

    def state_copy(d, s, slot):
        ref = states.at[slot, s]
        return pltpu.make_async_remote_copy(
            src_ref=ref, dst_ref=ref, send_sem=st_send.at[d - 1, s],
            recv_sem=st_recv.at[d - 1, s], device_id=(lax.rem(c + d, 4), h), device_id_type=MESH,
        )

    def local_states(s, carry):
        state = jnp.zeros((NS, channels), jnp.float32)
        for k in range(pk):
            j = s * pk + k
            if k > 0:
                part[s * (pk - 1) + k - 1] = state
            grown = dot(bu[j], xs[j], ((0,), (0,)))
            state = rows[j, 0:1, :] * state + rows[j, 1:2, :] * grown
        states[c, s] = state.astype(jnp.bfloat16)
        for d in range(1, 4):
            state_copy(d, s, c).start()
        return carry

    lax.fori_loop(0, seqs, local_states, 0)

    bc_copy(1, 1, far_slot, far).wait_recv()
    bc_copy(1, 2, far_slot, near).start()
    bc_copy(1, 0, near_slot, near).wait_recv()
    bc_copy(1, 2, cross_slot, near).wait_recv()
    lax.fori_loop(0, opts // 2 * ok, unfold_option, 0)

    for d in range(1, 4):
        dec_copy(d, lax.rem(c + 4 - d, 4)).wait_recv()
        for s in range(seqs):
            state_copy(d, s, lax.rem(c + 4 - d, 4)).wait_recv()

    skip = sg[...]
    skip = dot(
        jnp.concatenate(
            [
                skip.astype(jnp.bfloat16).astype(jnp.float32),
                skip - skip.astype(jnp.bfloat16).astype(jnp.float32),
                jnp.zeros((6, 8), jnp.float32),
            ],
            axis=0,
        ),
        (
            lax.broadcasted_iota(jnp.int32, (8, channels), 0)
            == lax.div(lax.broadcasted_iota(jnp.int32, (8, channels), 1), per_head)
        ).astype(jnp.float32),
    )
    skip = skip[0:1] + skip[1:2]

    def output(j, state, x, gate):
        scores = dot(cu[j], bu[j], ((1,), (1,)))
        scores = jnp.where(lower, scores, 0.0).astype(jnp.bfloat16)
        entering = (state * rows[j, 2:3, :]).astype(jnp.bfloat16)
        y = dot(scores, xs[j]) + dot(cu[j], entering)
        y = ee[j] * y + skip * x.astype(jnp.float32)
        return y * silu(gate.astype(jnp.float32))

    final = jnp.zeros((NS, channels), jnp.float32)
    for i in range(4):
        final = final * dec[i, pl.ds(c, 1), :] + states[i, c].astype(jnp.float32)
    mid[...] = final

    def option_out(o, carry):
        for k in range(ok):
            j = pchunks + o * ok + k
            state = mid[...]
            if k > 0:
                state = rows[j - 1, 0:1, :] * state + rows[j - 1, 1:2, :] * dot(
                    bu[j - 1], xs[j - 1], ((0,), (0,))
                )
            at = k * CHUNK
            ybufo[o, at : at + CHUNK, :] = output(
                j, state, xpado[o, HALO + at : HALO + at + CHUNK, :], go[o, at : at + CHUNK, :]
            )
        return carry

    loads[2].wait()
    loads[3].wait()
    lax.fori_loop(0, opts, option_out, 0)

    def prefix_out(s, carry):
        entering = jnp.zeros((NS, channels), jnp.float32)
        for i in range(3):
            step = entering * dec[i, pl.ds(s, 1), :] + states[i, s].astype(jnp.float32)
            entering = jnp.where(i < c, step, entering)
        mid[...] = entering
        factor = None
        for k in range(pk):
            j = s * pk + k
            state = mid[...]
            if k > 0:
                state = part[s * (pk - 1) + k - 1] + state * factor
            at = k * CHUNK
            ybuf[s, at : at + CHUNK, :] = output(
                j, state, xpad[s, HALO + at : HALO + at + CHUNK, :], gp[s, at : at + CHUNK, :]
            )
            factor = rows[j, 0:1, :] if k == 0 else factor * rows[j, 0:1, :]
        return carry

    lax.fori_loop(0, seqs, prefix_out, 0)

    pr, orr = tokens // nh, olen // nh

    def pack(i, carry):
        at = pl.multiple_of(2 * pr * i, 8)
        both = [ybuf[s, pl.ds(at, 2 * pr), :] for s in range(seqs)]
        for k in range(2):
            mine = [b[k * pr : (k + 1) * pr] for b in both]
            at_o = pl.multiple_of((2 * i + k) * orr, 8)
            mine += [ybufo[o, pl.ds(at_o, orr), :] for o in range(opts)]
            packed[2 * i + k] = jnp.concatenate(mine, axis=0).astype(jnp.bfloat16)
        return carry

    lax.fori_loop(0, nh // 2, pack, 0)

    for d in range(1, 4):
        rim_copy(d).wait_send()
        dec_copy(d, c).wait_send()
        for s in range(seqs):
            state_copy(d, s, c).wait_send()
    for part_no in range(2):
        bc_copy(part_no, 0, r, near).wait_send()
        bc_copy(part_no, 1, r, far).wait_send()
        bc_copy(part_no, 2, far_slot, near).wait_send()


def swap_kernel(heads, src, dst, own_sem, send_sem, recv_sem):
    c = lax.axis_index("ctx")
    h = lax.axis_index("head")
    own = pltpu.make_async_copy(src.at[h], dst.at[h], own_sem)
    own.start()
    barrier = pltpu.get_barrier_semaphore()

    def greet(d, carry):
        pl.semaphore_signal(
            barrier, 1, device_id=(c, lax.rem(h + d, heads)), device_id_type=MESH
        )
        return carry

    lax.fori_loop(1, heads, greet, 0)
    pl.semaphore_wait(barrier, heads - 1)

    def copy(d, target, slot):
        return pltpu.make_async_remote_copy(
            src_ref=src.at[target], dst_ref=dst.at[slot], send_sem=send_sem.at[d],
            recv_sem=recv_sem.at[d], device_id=(c, target), device_id_type=MESH,
        )

    def send(d, carry):
        copy(d, lax.rem(h + d, heads), h).start()
        return carry

    def finish(d, carry):
        copy(d, lax.rem(h + d, heads), h).wait_send()
        copy(d, lax.rem(h + d, heads), lax.rem(h + heads - d, heads)).wait_recv()
        return carry

    lax.fori_loop(1, heads, send, 0)
    lax.fori_loop(1, heads, finish, 0)
    own.wait()


def norm_kernel(seqs, pr, opts, orr, length, values, gain, prefix_out, option_out):
    h = lax.axis_index("head")
    blocks = [values[i].astype(jnp.float32) for i in range(4)]
    width = blocks[0].shape[1]
    total = sum(jnp.sum(b * b, axis=1, keepdims=True) for b in blocks)
    scale = lax.rsqrt(total / (4 * width) + EPSILON)
    first = seqs * pr
    place = lax.broadcasted_iota(jnp.int32, (orr, 1), 0) + h * orr
    for i in range(4):
        out = blocks[i] * scale * gain[:, i * width : (i + 1) * width]
        for s in range(seqs):
            prefix_out[s, :, i * width : (i + 1) * width] = out[s * pr : (s + 1) * pr].astype(jnp.bfloat16)
        for o in range(opts):
            keep = (place < length[o]).astype(jnp.float32)
            mine = out[first + o * orr : first + (o + 1) * orr] * keep
            option_out[o, :, i * width : (i + 1) * width] = mine.astype(jnp.bfloat16)


def per_device(
    prefix_x,
    prefix_bc,
    prefix_gate,
    prefix_steps,
    x_kernel,
    bc_kernel,
    step_bias,
    log_rate,
    skip_gain,
    norm_gain,
    option_x,
    option_bc,
    option_gate,
    option_steps,
    option_len,
):
    nh = lax.axis_size("head")
    seqs, tokens, channels = prefix_x.shape
    opts, olen = option_x.shape[0], option_x.shape[1]
    chunks = seqs * (tokens // CHUNK) + opts * (olen // CHUNK)
    half_rows = seqs // 2 * tokens + opts // 2 * olen
    pr, orr = tokens // nh, olen // nh
    block = seqs * pr + opts * orr
    bf16, f32 = jnp.bfloat16, jnp.float32
    anywhere = pl.BlockSpec(memory_space=pl.ANY)
    vmem = pl.BlockSpec(memory_space=pltpu.VMEM)
    dma = pltpu.SemaphoreType.DMA

    packed = pl.pallas_call(
        functools.partial(mixer_kernel, nh),
        out_shape=jax.ShapeDtypeStruct((nh, block, channels), bf16),
        in_specs=[anywhere, vmem, anywhere, vmem, anywhere, vmem, anywhere, vmem] + [vmem] * 5,
        out_specs=vmem,
        scratch_shapes=[
            pltpu.VMEM((seqs, HALO + tokens, channels), bf16),
            pltpu.VMEM((opts, HALO + olen, channels), bf16),
            pltpu.VMEM((seqs, tokens, channels), bf16),
            pltpu.VMEM((opts, olen, channels), bf16),
            pltpu.VMEM((4, HALO, channels + 128), bf16),
            pltpu.VMEM((4, half_rows, 128), bf16),
            pltpu.VMEM((4, seqs, NS, channels), bf16),
            pltpu.VMEM((4, 8, channels), f32),
            pltpu.VMEM((chunks, CHUNK, channels), bf16),
            pltpu.VMEM((chunks, CHUNK, channels), f32),
            pltpu.VMEM((chunks, 8, channels), f32),
            pltpu.VMEM((chunks, CHUNK, NS), bf16),
            pltpu.VMEM((chunks, CHUNK, NS), bf16),
            pltpu.VMEM((seqs * (tokens // CHUNK - 1), NS, channels), f32),
            pltpu.VMEM((NS, channels), f32),
            pltpu.VMEM((seqs, tokens, channels), f32),
            pltpu.VMEM((opts, olen, channels), f32),
            dma((4,)),
            dma((3,)), dma((3,)),
            dma((2, 3)), dma((2, 3)),
            dma((3, seqs)), dma((3, seqs)),
            dma((3,)), dma((3,)),
        ],
        compiler_params=pltpu.CompilerParams(
            collective_id=0, has_side_effects=True, vmem_limit_bytes=56 * MIB
        ),
        name="mixer",
    )(
        prefix_x, prefix_bc, prefix_gate, prefix_steps,
        option_x, option_bc, option_gate, option_steps,
        x_kernel, bc_kernel,
        step_bias.reshape(1, -1), log_rate.reshape(1, -1), skip_gain.reshape(1, -1),
    )

    swapped = pl.pallas_call(
        functools.partial(swap_kernel, nh),
        out_shape=jax.ShapeDtypeStruct((nh, block, channels), bf16),
        in_specs=[anywhere],
        out_specs=anywhere,
        scratch_shapes=[dma, dma((nh,)), dma((nh,))],
        compiler_params=pltpu.CompilerParams(collective_id=1, has_side_effects=True),
        name="swap",
    )(packed)

    group = 4 * channels
    inner = nh * channels
    return pl.pallas_call(
        functools.partial(norm_kernel, seqs, pr, opts, orr),
        grid_spec=pltpu.PrefetchScalarGridSpec(
            num_scalar_prefetch=1,
            grid=(nh // 4,),
            in_specs=[
                pl.BlockSpec((4, block, channels), lambda g, n: (g, 0, 0)),
                pl.BlockSpec((1, group), lambda g, n: (0, g)),
            ],
            out_specs=[
                pl.BlockSpec((seqs, pr, group), lambda g, n: (0, 0, g)),
                pl.BlockSpec((opts, orr, group), lambda g, n: (0, 0, g)),
            ],
        ),
        out_shape=[
            jax.ShapeDtypeStruct((seqs, pr, inner), bf16),
            jax.ShapeDtypeStruct((opts, orr, inner), bf16),
        ],
        compiler_params=pltpu.CompilerParams(vmem_limit_bytes=32 * MIB),
        name="norm",
    )(option_len, swapped, norm_gain.reshape(1, -1))


def solution(mesh):
    in_specs = (
        P(None, "ctx", "head"),
        P(None, "ctx", "head"),
        P(None, "ctx", "head"),
        P(None, "ctx", "head"),
        P(None, "head"),
        P(None, "head"),
        P("head"),
        P("head"),
        P("head"),
        P(),
        P("ctx", None, "head"),
        P("ctx", None, "head"),
        P("ctx", None, "head"),
        P("ctx", None, "head"),
        P("ctx"),
    )
    out_specs = (P(None, ("ctx", "head"), None), P("ctx", "head", None))
    return jax.shard_map(
        per_device, mesh=mesh, in_specs=in_specs, out_specs=out_specs, check_vma=False
    )
```

```python
import functools

import jax
import jax.numpy as jnp
from jax import lax
from jax.experimental import pallas as pl
from jax.experimental.pallas import tpu as pltpu
from jax.sharding import PartitionSpec as P

NS = 128
GROUPS = 8
CHUNK = 128
HALO = 16
EPSILON = 1e-05
MESH = pl.DeviceIdType.MESH
MIB = 1 << 20


def silu(v):
    return v / (1.0 + jnp.exp(-v))


def dot(a, b, dims=((1,), (0,)), precision=None):
    return lax.dot_general(
        a, b, (dims, ((), ())), precision=precision, preferred_element_type=jnp.float32
    )


def conv_window(window, taps, rows):
    total = window[HALO - 3 : HALO - 3 + rows] * taps[0:1]
    for k in range(1, 4):
        total = total + window[HALO - 3 + k : HALO - 3 + k + rows] * taps[k : k + 1]
    return silu(total)


def mixer_kernel(
    heads,
    px, pbc, pg, pst, ox, obc, og, ost, xk, bck, sb, lr, sg,
    out_p, out_o,
    xpad, xpado, gp, go, rim, gat, states, dec, xs, ee, rows, bu, cu, scores, part, ybuf, ybufo,
    pack_p, pack_o,
    load_sem, own_sem, rim_send, rim_recv, bc_send, bc_recv, ow_send, ow_recv, st_send, st_recv,
    dec_send, dec_recv, swap_send, swap_recv,
):
    c = lax.axis_index("ctx")
    h = lax.axis_index("head")
    seqs, tokens, channels = px.shape
    opts, olen = ox.shape[0], ox.shape[1]
    nh = heads
    pk, ok = tokens // CHUNK, olen // CHUNK
    pchunks, chunks = seqs * pk, seqs * pk + opts * ok
    cols = pbc.shape[1]
    half = channels // 2
    base = (h // 4) * 4
    r = lax.rem(h, 4)
    near = base + (r + 1 - 2 * lax.rem(r, 2))
    far = base + lax.rem(r + 2, 4)
    far_slot = lax.rem(r + 2, 4)
    near_slot = near - base
    cross_slot = lax.rem(near_slot + 2, 4)
    tops = (seqs // 2 + opts // 2) * HALO
    long_p, long_o = tokens - HALO, olen - HALO
    start_o = tops + seqs // 2 * long_p
    spans = ((0, tops), (tops, seqs // 2 * long_p), (start_o, opts // 2 * long_o))

    loads = [
        pltpu.make_async_copy(px, xpad.at[:, pl.ds(HALO, tokens), :], load_sem.at[0]),
        pltpu.make_async_copy(ox, xpado.at[:, pl.ds(HALO, olen), :], load_sem.at[1]),
        pltpu.make_async_copy(pg, gp, load_sem.at[2]),
        pltpu.make_async_copy(og, go, load_sem.at[3]),
    ]
    for load in loads:
        load.start()

    def partner(i):
        if nh != 32:
            return lax.rem(h + i, nh), lax.rem(h + nh - i, nh)
        z, y, k = h // 8, lax.rem(h // 2, 4), lax.rem(h, 2)
        dk, m = lax.rem(i, 2), i // 2
        dz, dy = lax.rem(m, 4), lax.rem(m // 4 + m, 4)
        core = lax.rem(k + dk, 2)
        to = lax.rem(z + dz, 4) * 8 + lax.rem(y + dy, 4) * 2 + core
        source = lax.rem(z + 4 - dz, 4) * 8 + lax.rem(y + 4 - dy, 4) * 2 + core
        return to, source

    barrier = pltpu.get_barrier_semaphore()

    def greet(i, carry):
        pl.semaphore_signal(barrier, 1, device_id=(c, lax.rem(h + i, nh)), device_id_type=MESH)
        return carry

    for d in range(1, 4):
        pl.semaphore_signal(barrier, 1, device_id=(lax.rem(c + d, 4), h), device_id_type=MESH)
    lax.fori_loop(1, nh, greet, 0)

    taps = bck[...].astype(jnp.float32)
    taps = jnp.concatenate([taps, taps], axis=1)
    blank = jnp.zeros((HALO, 2 * cols), jnp.float32)

    def pair(ref, a, count):
        both = jnp.concatenate([ref[a], ref[a + count // 2]], axis=0)
        return jnp.transpose(both.astype(jnp.float32))

    heads_p, heads_o, ends = [], [], []
    for a in range(seqs // 2):
        body = pair(pbc, a, seqs)
        heads_p.append(body[0:HALO])
        ends.append(body[tokens - 3 : tokens])
        out = conv_window(body, taps, long_p)
        gat[r, tops + a * long_p : tops + (a + 1) * long_p, :] = out.astype(jnp.bfloat16)
    for a in range(opts // 2):
        body = pair(obc, a, opts)
        heads_o.append(body[0:HALO])
        out = conv_window(body, taps, long_o)
        gat[r, start_o + a * long_o : start_o + (a + 1) * long_o, :] = out.astype(jnp.bfloat16)

    loads[0].wait()
    pad = jnp.zeros((HALO - 3 * seqs, channels), jnp.float32)
    tails = [xpad[s, tokens : tokens + HALO, :].astype(jnp.float32)[HALO - 3 :] for s in range(seqs)]
    rim[c, :, 0:channels] = jnp.concatenate(tails + [pad], axis=0).astype(jnp.bfloat16)
    pad = jnp.zeros((HALO - 3 * len(ends), 2 * cols), jnp.float32)
    rim[c, :, channels : channels + 2 * cols] = jnp.concatenate(ends + [pad], axis=0).astype(
        jnp.bfloat16
    )

    pl.semaphore_wait(barrier, nh + 2)

    def ctx_copy(ref, send, recv, d):
        return pltpu.make_async_remote_copy(
            src_ref=ref, dst_ref=ref, send_sem=send, recv_sem=recv,
            device_id=(lax.rem(c + d, 4), h), device_id_type=MESH,
        )

    def rim_copy(d, slot):
        return ctx_copy(rim.at[slot], rim_send.at[d - 1], rim_recv.at[d - 1], d)

    def bc_copy(part_no, way, slot, target):
        start, count = spans[part_no]
        ref = gat.at[slot, pl.ds(start, count), :]
        return pltpu.make_async_remote_copy(
            src_ref=ref, dst_ref=ref, send_sem=bc_send.at[part_no, way],
            recv_sem=bc_recv.at[part_no, way], device_id=(c, target), device_id_type=MESH,
        )

    for d in range(1, 4):
        rim_copy(d, c).start()
    for part_no in (1, 2):
        bc_copy(part_no, 1, r, far).start()
        bc_copy(part_no, 0, r, near).start()

    bias, rate = sb[...], -jnp.exp(lr[...])
    raw = [pst[s, :, k * CHUNK : (k + 1) * CHUNK] for s in range(seqs) for k in range(pk)]
    raw += [ost[o, :, k * CHUNK : (k + 1) * CHUNK] for o in range(opts) for k in range(ok)]
    raw += [jnp.zeros((256 - 8 * chunks, CHUNK), jnp.float32)]
    raw = jnp.transpose(jnp.concatenate(raw, axis=0))
    raw = raw + jnp.concatenate([bias] * 32, axis=1)
    size = jnp.maximum(raw, 0.0) + jnp.log1p(jnp.exp(-jnp.abs(raw)))
    move = size * jnp.concatenate([rate] * 32, axis=1)
    across = lax.broadcasted_iota(jnp.int32, (CHUNK, CHUNK), 0)
    along = lax.broadcasted_iota(jnp.int32, (CHUNK, CHUNK), 1)
    lower = across >= along
    cumul = dot(lower.astype(jnp.float32), move, precision=lax.Precision.HIGHEST)
    middle, end = cumul[CHUNK // 2 - 1 : CHUNK // 2], cumul[CHUNK - 1 : CHUNK]
    filler = jnp.zeros((13, end.shape[1]), jnp.float32)
    wide = jnp.concatenate(
        [
            jnp.exp(middle - cumul) * size,
            jnp.exp(cumul - middle),
            jnp.exp(end),
            jnp.exp(end - middle),
            jnp.exp(middle),
            filler,
        ],
        axis=0,
    )
    wide_high = wide.astype(jnp.bfloat16)
    wide_low = (wide - wide_high.astype(jnp.float32)).astype(jnp.bfloat16)
    lanes = wide.shape[1]
    per_head = channels // 8
    spread_row = lax.broadcasted_iota(jnp.int32, (lanes, channels), 0)
    spread_head = lax.div(lax.broadcasted_iota(jnp.int32, (lanes, channels), 1), per_head)

    xtaps = xk[...].astype(jnp.float32)

    def convolve(j, window):
        out = conv_window(window, xtaps, CHUNK).astype(jnp.bfloat16)
        pick = (spread_row == 8 * j + spread_head).astype(jnp.bfloat16)
        grown = dot(wide_high, pick) + dot(wide_low, pick)
        xs[j] = (out.astype(jnp.float32) * grown[0:CHUNK]).astype(jnp.bfloat16)
        ee[j] = grown[CHUNK : 2 * CHUNK]
        rows[j] = grown[2 * CHUNK : 2 * CHUNK + 8]
        return out

    def prefix_conv(s, k):
        at = k * CHUNK if isinstance(k, int) else pl.multiple_of(k * CHUNK, CHUNK)
        window = xpad[s, pl.ds(at, CHUNK + HALO), :].astype(jnp.float32)
        xpad[s, pl.ds(at + HALO, CHUNK), :] = convolve(s * pk + k, window)

    def option_conv(i, carry):
        o, k = i // ok, ok - 1 - lax.rem(i, ok)
        at = pl.multiple_of(k * CHUNK, CHUNK)
        window = xpado[o, pl.ds(at, CHUNK + HALO), :].astype(jnp.float32)
        xpado[o, pl.ds(at + HALO, CHUNK), :] = convolve(pchunks + o * ok + k, window)
        return carry

    def later_chunks(i, carry):
        prefix_conv(i // (pk - 1), pk - 1 - lax.rem(i, pk - 1))
        return carry

    def first_chunks(s, carry):
        prefix_conv(s, 0)
        return carry

    for d in range(1, 4):
        rim_copy(d, lax.rem(c + 4 - d, 4)).wait_recv()
    before = rim[lax.rem(c + 3, 4)].astype(jnp.float32) * (c > 0).astype(jnp.float32)
    last = rim[3].astype(jnp.float32)
    zeros = jnp.zeros((HALO - 3, channels), jnp.float32)
    owner_tail = jnp.zeros((3, channels), jnp.float32)
    owner_bc = jnp.zeros((3, cols), jnp.float32)
    for s in range(seqs):
        mine = (c == s).astype(jnp.float32)
        tail = before[3 * s : 3 * s + 3, 0:channels]
        xpad[s, 0:HALO, :] = jnp.concatenate([zeros, tail], axis=0).astype(jnp.bfloat16)
        owner_tail = owner_tail + last[3 * s : 3 * s + 3, 0:channels] * mine
        a, side = s % (seqs // 2), channels + cols * (s // (seqs // 2))
        owner_bc = owner_bc + last[3 * a : 3 * a + 3, side : side + cols] * mine
    loads[1].wait()
    for o in range(opts):
        xpado[o, 0:HALO, :] = jnp.concatenate([zeros, owner_tail], axis=0).astype(jnp.bfloat16)
    zeros = jnp.zeros((HALO - 3, 2 * cols), jnp.float32)
    for a in range(seqs // 2):
        tail = before[3 * a : 3 * a + 3, channels : channels + 2 * cols]
        window = jnp.concatenate([zeros, tail, heads_p[a]], axis=0)
        gat[r, a * HALO : (a + 1) * HALO, :] = conv_window(window, taps, HALO).astype(jnp.bfloat16)
    tail = jnp.concatenate([owner_bc, owner_bc], axis=1)
    for a in range(opts // 2):
        at = (seqs // 2 + a) * HALO
        window = jnp.concatenate([zeros, tail, heads_o[a]], axis=0)
        gat[r, at : at + HALO, :] = conv_window(window, taps, HALO).astype(jnp.bfloat16)
    bc_copy(0, 1, r, far).start()
    bc_copy(0, 0, r, near).start()

    lax.fori_loop(0, seqs * (pk - 1), later_chunks, 0)

    for part_no in (1, 0):
        bc_copy(part_no, 1, far_slot, far).wait_recv()
        bc_copy(part_no, 2, far_slot, near).start()

    lax.fori_loop(0, seqs, first_chunks, 0)

    for s in range(seqs):
        total = rows[s * pk, 0:1, :]
        for k in range(1, pk):
            total = total * rows[s * pk + k, 0:1, :]
        dec[c, s : s + 1, :] = total

    def dec_copy(d, slot):
        return ctx_copy(dec.at[slot], dec_send.at[d - 1], dec_recv.at[d - 1], d)

    for d in range(1, 4):
        dec_copy(d, c).start()

    left = lax.broadcasted_iota(jnp.int32, (CHUNK, 128), 1) < 64

    def unfold(top, start, low, high):
        if top is None:
            parts = [gat[i, pl.ds(start, CHUNK), :].astype(jnp.float32) for i in range(4)]
        else:
            parts = [
                jnp.concatenate(
                    [gat[i, pl.ds(top, HALO), :], gat[i, pl.ds(start, CHUNK - HALO), :]], axis=0
                ).astype(jnp.float32)
                for i in range(4)
            ]
        turned = [pltpu.roll(p, 64, 1) for p in parts]
        bu[low] = jnp.where(left, parts[0], turned[1]).astype(jnp.bfloat16)
        bu[high] = jnp.where(left, turned[0], parts[1]).astype(jnp.bfloat16)
        cu[low] = jnp.where(left, parts[2], turned[3]).astype(jnp.bfloat16)
        cu[high] = jnp.where(left, turned[2], parts[3]).astype(jnp.bfloat16)
        for j in (low, high):
            raw_scores = dot(cu[j], bu[j], ((1,), (1,)))
            scores[j] = jnp.where(lower, raw_scores, 0.0).astype(jnp.bfloat16)

    def unfold_prefix(a, carry):
        for k in range(pk):
            top = None if k else pl.multiple_of(a * HALO, HALO)
            start = tops + a * long_p + max(k * CHUNK - HALO, 0)
            unfold(top, pl.multiple_of(start, HALO), a * pk + k, (a + seqs // 2) * pk + k)
        return carry

    def unfold_option(a, carry):
        for k in range(ok):
            top = None if k else pl.multiple_of((seqs // 2 + a) * HALO, HALO)
            start = start_o + a * long_o + max(k * CHUNK - HALO, 0)
            unfold(
                top, pl.multiple_of(start, HALO),
                pchunks + a * ok + k, pchunks + (a + opts // 2) * ok + k,
            )
        return carry

    for part_no in (1, 0):
        bc_copy(part_no, 0, near_slot, near).wait_recv()
        bc_copy(part_no, 2, cross_slot, near).wait_recv()
    lax.fori_loop(0, seqs // 2, unfold_prefix, 0)

    def owner_copy(d, side, s, slot):
        return ctx_copy(
            states.at[slot, side, s], ow_send.at[d - 1, side], ow_recv.at[d - 1, side], d
        )

    def state_copy(d, side, n, s, slot):
        return ctx_copy(
            states.at[slot, side, s], st_send.at[d - 1, side, n], st_recv.at[d - 1, side, n], d
        )

    for d in range(1, 5):
        s = lax.rem(c + d, 4)
        state = jnp.zeros((NS, channels), jnp.float32)
        for k in range(pk):
            j = s * pk + k
            if k > 0:
                part[s * (pk - 1) + k - 1] = state
            grown = dot(bu[j], xs[j], ((0,), (0,)))
            state = rows[j, 0:1, :] * state + rows[j, 1:2, :] * grown
        for side in range(2):
            states[c, side, s] = state[:, side * half : (side + 1) * half].astype(jnp.bfloat16)
            if d < 4:
                owner_copy(d, side, s, c).start()

    def each_later(side, act):
        for d in range(1, 4):

            @pl.when(c + d < 4)
            def _():
                for n in range(3):
                    act(state_copy(d, side, n, lax.rem(c + d + 1 + n, 4), c))

    for side in range(2):
        each_later(side, lambda copy: copy.start())

    bc_copy(2, 1, far_slot, far).wait_recv()
    bc_copy(2, 2, far_slot, near).start()
    lax.fori_loop(0, opts * ok, option_conv, 0)
    bc_copy(2, 0, near_slot, near).wait_recv()
    bc_copy(2, 2, cross_slot, near).wait_recv()
    lax.fori_loop(0, opts // 2, unfold_option, 0)

    skip = sg[...]
    skip = dot(
        jnp.concatenate(
            [
                skip.astype(jnp.bfloat16).astype(jnp.float32),
                skip - skip.astype(jnp.bfloat16).astype(jnp.float32),
                jnp.zeros((6, 8), jnp.float32),
            ],
            axis=0,
        ),
        (
            lax.broadcasted_iota(jnp.int32, (8, channels), 0)
            == lax.div(lax.broadcasted_iota(jnp.int32, (8, channels), 1), per_head)
        ).astype(jnp.float32),
    )
    skip = skip[0:1] + skip[1:2]

    def output(j, lo, state, x, gate):
        at = slice(lo, lo + half)
        entering = (state * rows[j, 2:3, at]).astype(jnp.bfloat16)
        y = dot(scores[j], xs[j, :, at]) + dot(cu[j], entering)
        y = ee[j, :, at] * y + skip[:, at] * x.astype(jnp.float32)
        return y * silu(gate.astype(jnp.float32))

    pr, orr = tokens // nh, olen // nh

    def swap_copy(kind, side, i, slot_from, slot_to):
        packed, out = ((pack_o, out_o), (pack_p, out_p))[kind]
        to, _ = partner(i)
        return pltpu.make_async_remote_copy(
            src_ref=packed.at[side, slot_from], dst_ref=out.at[side, slot_to],
            send_sem=swap_send.at[kind, side, i], recv_sem=swap_recv.at[kind, side, i],
            device_id=(c, to), device_id_type=MESH,
        )

    def own_copy(kind, side):
        packed, out = ((pack_o, out_o), (pack_p, out_p))[kind]
        return pltpu.make_async_copy(packed.at[side, h], out.at[side, h], own_sem.at[kind, side])

    def send_all(kind, side):
        def send(i, carry):
            to, _ = partner(i)
            swap_copy(kind, side, i, to, h).start()
            return carry

        own_copy(kind, side).start()
        lax.fori_loop(1, nh, send, 0)

    def finish(kind, side):
        def one(i, carry):
            to, source = partner(i)
            swap_copy(kind, side, i, to, h).wait_send()
            swap_copy(kind, side, i, source, source).wait_recv()
            return carry

        own_copy(kind, side).wait()
        lax.fori_loop(1, nh, one, 0)

    for d in range(1, 4):
        dec_copy(d, lax.rem(c + 4 - d, 4)).wait_recv()
    loads[2].wait()
    loads[3].wait()
    for side in range(2):
        lo = side * half
        at = slice(lo, lo + half)
        for d in range(1, 4):
            owner_copy(d, side, c, lax.rem(c + 4 - d, 4)).wait_recv()
        final = jnp.zeros((NS, half), jnp.float32)
        for i in range(4):
            final = final * dec[i, pl.ds(c, 1), at] + states[i, side, c].astype(jnp.float32)

        def option_out(o, carry, side=side, lo=lo, at=at, final=final):
            state = final
            for k in range(ok):
                j = pchunks + o * ok + k
                if k > 0:
                    grown = dot(bu[j - 1], xs[j - 1, :, at], ((0,), (0,)))
                    state = rows[j - 1, 0:1, at] * state + rows[j - 1, 1:2, at] * grown
                p = k * CHUNK
                m = output(
                    j, lo, state, xpado[o, HALO + p : HALO + p + CHUNK, at], go[o, p : p + CHUNK, at]
                )
                some = CHUNK // orr
                ybufo[k * some : (k + 1) * some, pl.ds(pl.multiple_of(o * orr, 8), orr), :] = (
                    m.reshape(some, orr, half)
                )
            return carry

        lax.fori_loop(0, opts, option_out, 0)
        for i in range(nh):
            pack_o[side, i] = ybufo[i].astype(jnp.bfloat16)
        send_all(0, side)

    for side in range(2):
        lo = side * half
        at = slice(lo, lo + half)
        for d in range(1, 4):

            @pl.when(c >= d)
            def _():
                for n in range(3):
                    s = lax.rem(c + 1 + n, 4)
                    state_copy(d, side, n, s, lax.rem(c + 4 - d, 4)).wait_recv()

        def prefix_out(s, carry, side=side, lo=lo, at=at):
            state = jnp.zeros((NS, half), jnp.float32)
            for i in range(3):
                step = state * dec[i, pl.ds(s, 1), at] + states[i, side, s].astype(jnp.float32)
                state = jnp.where(i < c, step, state)
            factor = jnp.ones((1, half), jnp.float32)
            for k in range(pk):
                j = s * pk + k
                now = state if k == 0 else part[s * (pk - 1) + k - 1, :, at] + state * factor
                p = k * CHUNK
                m = output(
                    j, lo, now, xpad[s, HALO + p : HALO + p + CHUNK, at], gp[s, p : p + CHUNK, at]
                )
                for n in range(half // 128):
                    ybuf[n, pl.ds(seqs * p + s, CHUNK, seqs), :] = m[:, n * 128 : (n + 1) * 128]
                factor = factor * rows[j, 0:1, at]
            return carry

        lax.fori_loop(0, seqs, prefix_out, 0)

        def pack(i, carry, side=side):
            start = pl.multiple_of(i * seqs * pr, 16)
            for n in range(half // 128):
                pack_p[side, i, :, n * 128 : (n + 1) * 128] = ybuf[
                    n, pl.ds(start, seqs * pr), :
                ].astype(jnp.bfloat16)
            return carry

        lax.fori_loop(0, nh, pack, 0)
        send_all(1, side)

    for d in range(1, 4):
        rim_copy(d, c).wait_send()
        dec_copy(d, c).wait_send()
        for side in range(2):
            owner_copy(d, side, lax.rem(c + d, 4), c).wait_send()
    for side in range(2):
        each_later(side, lambda copy: copy.wait_send())
    for part_no in range(3):
        bc_copy(part_no, 0, r, near).wait_send()
        bc_copy(part_no, 1, r, far).wait_send()
        bc_copy(part_no, 2, far_slot, near).wait_send()
    for kind in range(2):
        for side in range(2):
            finish(kind, side)


def norm_kernel(seqs, pr, opts, orr, length, values_p, values_o, gain, prefix_out, option_out):
    h = lax.axis_index("head")
    half = values_p.shape[3]
    place = lax.broadcasted_iota(jnp.int32, (orr, 1), 0) + h * orr

    def scaled(values):
        blocks = [values[side, i].astype(jnp.float32) for i in range(4) for side in range(2)]
        total = sum(jnp.sum(b * b, axis=1, keepdims=True) for b in blocks)
        scale = lax.rsqrt(total / (8 * half) + EPSILON)
        return [b * scale * gain[:, n * half : (n + 1) * half] for n, b in enumerate(blocks)]

    for n, out in enumerate(scaled(values_p)):
        at = slice(n * half, (n + 1) * half)
        for i in range(pr):
            prefix_out[i, :, at] = out[i * seqs : (i + 1) * seqs].astype(jnp.bfloat16)
    keeps = [(place < length[o]).astype(jnp.float32) for o in range(opts)]
    for n, out in enumerate(scaled(values_o)):
        at = slice(n * half, (n + 1) * half)
        for o in range(opts):
            mine = out[o * orr : (o + 1) * orr] * keeps[o]
            option_out[o, :, at] = mine.astype(jnp.bfloat16)


def per_device(
    prefix_x,
    prefix_bc,
    prefix_gate,
    prefix_steps,
    x_kernel,
    bc_kernel,
    step_bias,
    log_rate,
    skip_gain,
    norm_gain,
    option_x,
    option_bc,
    option_gate,
    option_steps,
    option_len,
):
    nh = lax.axis_size("head")
    seqs, tokens, channels = prefix_x.shape
    opts, olen = option_x.shape[0], option_x.shape[1]
    chunks = seqs * (tokens // CHUNK) + opts * (olen // CHUNK)
    half_rows = seqs // 2 * tokens + opts // 2 * olen
    half = channels // 2
    pr, orr = tokens // nh, olen // nh
    bf16, f32 = jnp.bfloat16, jnp.float32
    anywhere = pl.BlockSpec(memory_space=pl.ANY)
    vmem = pl.BlockSpec(memory_space=pltpu.VMEM)
    dma = pltpu.SemaphoreType.DMA
    flip = functools.partial(jnp.swapaxes, axis1=1, axis2=2)

    swapped_p, swapped_o = pl.pallas_call(
        functools.partial(mixer_kernel, nh),
        out_shape=[
            jax.ShapeDtypeStruct((2, nh, seqs * pr, half), bf16),
            jax.ShapeDtypeStruct((2, nh, opts * orr, half), bf16),
        ],
        in_specs=[anywhere, vmem, anywhere, vmem, anywhere, vmem, anywhere, vmem] + [vmem] * 5,
        out_specs=[vmem, vmem],
        scratch_shapes=[
            pltpu.VMEM((seqs, HALO + tokens, channels), bf16),
            pltpu.VMEM((opts, HALO + olen, channels), bf16),
            pltpu.VMEM((seqs, tokens, channels), bf16),
            pltpu.VMEM((opts, olen, channels), bf16),
            pltpu.VMEM((4, HALO, channels + 128), bf16),
            pltpu.VMEM((4, half_rows, 128), bf16),
            pltpu.VMEM((4, 2, seqs, NS, half), bf16),
            pltpu.VMEM((4, 8, channels), f32),
            pltpu.VMEM((chunks, CHUNK, channels), bf16),
            pltpu.VMEM((chunks, CHUNK, channels), f32),
            pltpu.VMEM((chunks, 8, channels), f32),
            pltpu.VMEM((chunks, CHUNK, NS), bf16),
            pltpu.VMEM((chunks, CHUNK, NS), bf16),
            pltpu.VMEM((chunks, CHUNK, CHUNK), bf16),
            pltpu.VMEM((seqs * (tokens // CHUNK - 1), NS, channels), f32),
            pltpu.VMEM((half // 128, seqs * tokens, 128), f32),
            pltpu.VMEM((nh, opts * orr, half), f32),
            pltpu.VMEM((2, nh, seqs * pr, half), bf16),
            pltpu.VMEM((2, nh, opts * orr, half), bf16),
            dma((4,)),
            dma((2, 2)),
            dma((3,)), dma((3,)),
            dma((3, 3)), dma((3, 3)),
            dma((3, 2)), dma((3, 2)),
            dma((3, 2, 3)), dma((3, 2, 3)),
            dma((3,)), dma((3,)),
            dma((2, 2, nh)), dma((2, 2, nh)),
        ],
        compiler_params=pltpu.CompilerParams(
            collective_id=0, has_side_effects=True, vmem_limit_bytes=56 * MIB
        ),
        name="mixer",
    )(
        prefix_x, flip(prefix_bc), prefix_gate, flip(prefix_steps),
        option_x, flip(option_bc), option_gate, flip(option_steps),
        x_kernel, bc_kernel,
        step_bias.reshape(1, -1), log_rate.reshape(1, -1), skip_gain.reshape(1, -1),
    )

    group = 4 * channels
    inner = nh * channels
    prefix_out, option_out = pl.pallas_call(
        functools.partial(norm_kernel, seqs, pr, opts, orr),
        grid_spec=pltpu.PrefetchScalarGridSpec(
            num_scalar_prefetch=1,
            grid=(nh // 4,),
            in_specs=[
                pl.BlockSpec((2, 4, seqs * pr, half), lambda g, n: (0, g, 0, 0)),
                pl.BlockSpec((2, 4, opts * orr, half), lambda g, n: (0, g, 0, 0)),
                pl.BlockSpec((1, group), lambda g, n: (0, g)),
            ],
            out_specs=[
                pl.BlockSpec((pr, seqs, group), lambda g, n: (0, 0, g)),
                pl.BlockSpec((opts, orr, group), lambda g, n: (0, 0, g)),
            ],
        ),
        out_shape=[
            jax.ShapeDtypeStruct((pr, seqs, inner), bf16),
            jax.ShapeDtypeStruct((opts, orr, inner), bf16),
        ],
        compiler_params=pltpu.CompilerParams(vmem_limit_bytes=32 * MIB),
        name="norm",
    )(option_len, swapped_p, swapped_o, norm_gain.reshape(1, -1))
    return jnp.swapaxes(prefix_out, 0, 1), option_out


def solution(mesh):
    in_specs = (
        P(None, "ctx", "head"),
        P(None, "ctx", "head"),
        P(None, "ctx", "head"),
        P(None, "ctx", "head"),
        P(None, "head"),
        P(None, "head"),
        P("head"),
        P("head"),
        P("head"),
        P(),
        P("ctx", None, "head"),
        P("ctx", None, "head"),
        P("ctx", None, "head"),
        P("ctx", None, "head"),
        P("ctx"),
    )
    out_specs = (P(None, ("ctx", "head"), None), P("ctx", "head", None))
    return jax.shard_map(
        per_device, mesh=mesh, in_specs=in_specs, out_specs=out_specs, check_vma=False
    )
```

```python
import functools

import jax
import jax.numpy as jnp
from jax import lax
from jax.experimental import pallas as pl
from jax.experimental.pallas import tpu as pltpu
from jax.sharding import PartitionSpec as P

NS = 128
GROUPS = 8
CHUNK = 128
HALO = 16
EPSILON = 1e-05
MESH = pl.DeviceIdType.MESH
MIB = 1 << 20


def silu(v):
    return v / (1.0 + jnp.exp(-v))


def dot(a, b, dims=((1,), (0,)), precision=None):
    return lax.dot_general(
        a, b, (dims, ((), ())), precision=precision, preferred_element_type=jnp.float32
    )


def conv_window(window, taps, rows):
    total = window[HALO - 3 : HALO - 3 + rows] * taps[0:1]
    for k in range(1, 4):
        total = total + window[HALO - 3 + k : HALO - 3 + k + rows] * taps[k : k + 1]
    return silu(total)


def mixer_kernel(
    heads,
    px, pbc, pg, pst, ox, obc, og, ost, xk, bck, sb, lr, sg,
    out_p, out_o,
    xpad, xpado, gp, go, rim, gat, states, dec, xs, ee, rows, bu, cu, scores, part, ybuf, ybufo,
    pack_p, pack_o,
    load_sem, own_sem, rim_send, rim_recv, bc_send, bc_recv, ow_send, ow_recv, st_send, st_recv,
    dec_send, dec_recv, swap_send, swap_recv,
):
    c = lax.axis_index("ctx")
    h = lax.axis_index("head")
    seqs, tokens, channels = px.shape
    opts, olen = ox.shape[0], ox.shape[1]
    nh = heads
    pk, ok = tokens // CHUNK, olen // CHUNK
    pchunks, chunks = seqs * pk, seqs * pk + opts * ok
    cols = pbc.shape[1]
    half = channels // 2
    base = (h // 4) * 4
    r = lax.rem(h, 4)
    near = base + (r + 1 - 2 * lax.rem(r, 2))
    far = base + lax.rem(r + 2, 4)
    far_slot = lax.rem(r + 2, 4)
    near_slot = near - base
    cross = base + lax.rem(near_slot + 2, 4)
    cross_slot = lax.rem(near_slot + 2, 4)
    tops = (seqs // 2 + opts // 2) * HALO
    long_p, long_o = tokens - HALO, olen - HALO
    start_o = tops + seqs // 2 * long_p
    spans = ((0, tops), (tops, seqs // 2 * long_p), (start_o, opts // 2 * long_o))

    loads = [
        pltpu.make_async_copy(px, xpad.at[:, pl.ds(HALO, tokens), :], load_sem.at[0]),
        pltpu.make_async_copy(ox, xpado.at[:, pl.ds(HALO, olen), :], load_sem.at[1]),
        pltpu.make_async_copy(pg, gp, load_sem.at[2]),
        pltpu.make_async_copy(og, go, load_sem.at[3]),
    ]
    for load in loads:
        load.start()

    def partner(i):
        if nh != 32:
            return lax.rem(h + i, nh)
        z, y, k = h // 8, lax.rem(h // 2, 4), lax.rem(h, 2)
        dk, m = lax.rem(i, 2), i // 2
        dz, dy = lax.rem(m, 4), lax.rem(m // 4 + m, 4)
        core = lax.rem(k + dk, 2)
        return lax.rem(z + dz, 4) * 8 + lax.rem(y + dy, 4) * 2 + core

    barrier = pltpu.get_barrier_semaphore()

    def greet(i, carry):
        pl.semaphore_signal(barrier, 1, device_id=(c, lax.rem(h + i, nh)), device_id_type=MESH)
        return carry

    for d in range(1, 4):
        pl.semaphore_signal(barrier, 1, device_id=(lax.rem(c + d, 4), h), device_id_type=MESH)
    lax.fori_loop(1, nh, greet, 0)

    taps = bck[...].astype(jnp.float32)
    taps = jnp.concatenate([taps, taps], axis=1)
    blank = jnp.zeros((HALO, 2 * cols), jnp.float32)

    def pair(ref, a, count):
        both = jnp.concatenate([ref[a], ref[a + count // 2]], axis=0)
        return jnp.transpose(both.astype(jnp.float32))

    heads_p, heads_o, ends = [], [], []
    for a in range(seqs // 2):
        body = pair(pbc, a, seqs)
        heads_p.append(body[0:HALO])
        ends.append(body[tokens - 3 : tokens])
        out = conv_window(body, taps, long_p)
        gat[r, tops + a * long_p : tops + (a + 1) * long_p, :] = out.astype(jnp.bfloat16)
    for a in range(opts // 2):
        body = pair(obc, a, opts)
        heads_o.append(body[0:HALO])
        out = conv_window(body, taps, long_o)
        gat[r, start_o + a * long_o : start_o + (a + 1) * long_o, :] = out.astype(jnp.bfloat16)

    loads[0].wait()
    pad = jnp.zeros((HALO - 3 * seqs, channels), jnp.float32)
    tails = [xpad[s, tokens : tokens + HALO, :].astype(jnp.float32)[HALO - 3 :] for s in range(seqs)]
    rim[c, :, 0:channels] = jnp.concatenate(tails + [pad], axis=0).astype(jnp.bfloat16)
    pad = jnp.zeros((HALO - 3 * len(ends), 2 * cols), jnp.float32)
    rim[c, :, channels : channels + 2 * cols] = jnp.concatenate(ends + [pad], axis=0).astype(
        jnp.bfloat16
    )

    pl.semaphore_wait(barrier, nh + 2)

    def ctx_copy(ref, send, recv, d):
        return pltpu.make_async_remote_copy(
            src_ref=ref, dst_ref=ref, send_sem=send, recv_sem=recv,
            device_id=(lax.rem(c + d, 4), h), device_id_type=MESH,
        )

    def rim_copy(d, slot):
        return ctx_copy(rim.at[slot], rim_send.at[0], rim_recv.at[d - 1], d)

    def bc_copy(part_no, way, slot, target):
        start, count = spans[part_no]
        ref = gat.at[slot, pl.ds(start, count), :]
        return pltpu.make_async_remote_copy(
            src_ref=ref, dst_ref=ref, send_sem=bc_send.at[0],
            recv_sem=bc_recv.at[part_no, way], device_id=(c, target), device_id_type=MESH,
        )

    for d in range(1, 4):
        rim_copy(d, c).start()
    bc_copy(1, 1, r, far).start()
    bc_copy(1, 0, r, near).start()

    bias, rate = sb[...], -jnp.exp(lr[...])
    raw = [pst[s, :, k * CHUNK : (k + 1) * CHUNK] for s in range(seqs) for k in range(pk)]
    raw += [ost[o, :, k * CHUNK : (k + 1) * CHUNK] for o in range(opts) for k in range(ok)]
    raw += [jnp.zeros((256 - 8 * chunks, CHUNK), jnp.float32)]
    raw = jnp.transpose(jnp.concatenate(raw, axis=0))
    raw = raw + jnp.concatenate([bias] * 32, axis=1)
    size = jnp.maximum(raw, 0.0) + jnp.log1p(jnp.exp(-jnp.abs(raw)))
    move = size * jnp.concatenate([rate] * 32, axis=1)
    across = lax.broadcasted_iota(jnp.int32, (CHUNK, CHUNK), 0)
    along = lax.broadcasted_iota(jnp.int32, (CHUNK, CHUNK), 1)
    lower = across >= along
    cumul = dot(lower.astype(jnp.float32), move, precision=lax.Precision.HIGHEST)
    middle, end = cumul[CHUNK // 2 - 1 : CHUNK // 2], cumul[CHUNK - 1 : CHUNK]
    filler = jnp.zeros((13, end.shape[1]), jnp.float32)
    wide = jnp.concatenate(
        [
            jnp.exp(middle - cumul) * size,
            jnp.exp(cumul - middle),
            jnp.exp(end),
            jnp.exp(end - middle),
            jnp.exp(middle),
            filler,
        ],
        axis=0,
    )
    wide_high = wide.astype(jnp.bfloat16)
    wide_low = (wide - wide_high.astype(jnp.float32)).astype(jnp.bfloat16)
    lanes = wide.shape[1]
    per_head = channels // 8
    spread_row = lax.broadcasted_iota(jnp.int32, (lanes, channels), 0)
    spread_head = lax.div(lax.broadcasted_iota(jnp.int32, (lanes, channels), 1), per_head)

    xtaps = xk[...].astype(jnp.float32)

    def convolve(j, window):
        out = conv_window(window, xtaps, CHUNK).astype(jnp.bfloat16)
        pick = (spread_row == 8 * j + spread_head).astype(jnp.bfloat16)
        grown = dot(wide_high, pick) + dot(wide_low, pick)
        xs[j] = (out.astype(jnp.float32) * grown[0:CHUNK]).astype(jnp.bfloat16)
        ee[j] = grown[CHUNK : 2 * CHUNK]
        rows[j] = grown[2 * CHUNK : 2 * CHUNK + 8]
        return out

    def prefix_conv(s, k):
        at = k * CHUNK if isinstance(k, int) else pl.multiple_of(k * CHUNK, CHUNK)
        window = xpad[s, pl.ds(at, CHUNK + HALO), :].astype(jnp.float32)
        xpad[s, pl.ds(at + HALO, CHUNK), :] = convolve(s * pk + k, window)

    def option_conv(i, carry):
        o, k = i // ok, ok - 1 - lax.rem(i, ok)
        at = pl.multiple_of(k * CHUNK, CHUNK)
        window = xpado[o, pl.ds(at, CHUNK + HALO), :].astype(jnp.float32)
        xpado[o, pl.ds(at + HALO, CHUNK), :] = convolve(pchunks + o * ok + k, window)
        return carry

    def later_chunks(i, carry):
        prefix_conv(i // (pk - 1), pk - 1 - lax.rem(i, pk - 1))
        return carry

    def first_chunks(s, carry):
        prefix_conv(s, 0)
        return carry

    for d in range(1, 4):
        rim_copy(d, lax.rem(c + 4 - d, 4)).wait_recv()
    before = rim[lax.rem(c + 3, 4)].astype(jnp.float32) * (c > 0).astype(jnp.float32)
    last = rim[3].astype(jnp.float32)
    zeros = jnp.zeros((HALO - 3, channels), jnp.float32)
    owner_tail = jnp.zeros((3, channels), jnp.float32)
    owner_bc = jnp.zeros((3, cols), jnp.float32)
    for s in range(seqs):
        mine = (c == s).astype(jnp.float32)
        tail = before[3 * s : 3 * s + 3, 0:channels]
        xpad[s, 0:HALO, :] = jnp.concatenate([zeros, tail], axis=0).astype(jnp.bfloat16)
        owner_tail = owner_tail + last[3 * s : 3 * s + 3, 0:channels] * mine
        a, side = s % (seqs // 2), channels + cols * (s // (seqs // 2))
        owner_bc = owner_bc + last[3 * a : 3 * a + 3, side : side + cols] * mine
    loads[1].wait()
    for o in range(opts):
        xpado[o, 0:HALO, :] = jnp.concatenate([zeros, owner_tail], axis=0).astype(jnp.bfloat16)
    zeros = jnp.zeros((HALO - 3, 2 * cols), jnp.float32)
    for a in range(seqs // 2):
        tail = before[3 * a : 3 * a + 3, channels : channels + 2 * cols]
        window = jnp.concatenate([zeros, tail, heads_p[a]], axis=0)
        gat[r, a * HALO : (a + 1) * HALO, :] = conv_window(window, taps, HALO).astype(jnp.bfloat16)
    tail = jnp.concatenate([owner_bc, owner_bc], axis=1)
    for a in range(opts // 2):
        at = (seqs // 2 + a) * HALO
        window = jnp.concatenate([zeros, tail, heads_o[a]], axis=0)
        gat[r, at : at + HALO, :] = conv_window(window, taps, HALO).astype(jnp.bfloat16)
    bc_copy(0, 1, r, far).start()
    bc_copy(0, 2, r, cross).start()
    bc_copy(0, 0, r, near).start()
    bc_copy(2, 1, r, far).start()
    bc_copy(2, 0, r, near).start()

    lax.fori_loop(0, seqs * (pk - 1), later_chunks, 0)

    bc_copy(1, 1, far_slot, far).wait_recv()
    bc_copy(1, 2, far_slot, near).start()

    lax.fori_loop(0, seqs, first_chunks, 0)

    for s in range(seqs):
        total = rows[s * pk, 0:1, :]
        for k in range(1, pk):
            total = total * rows[s * pk + k, 0:1, :]
        dec[c, s : s + 1, :] = total

    def dec_copy(d, slot):
        return ctx_copy(dec.at[slot], dec_send.at[0], dec_recv.at[d - 1], d)

    for d in range(1, 4):
        dec_copy(d, c).start()

    left = lax.broadcasted_iota(jnp.int32, (CHUNK, 128), 1) < 64

    def unfold(to, first, top, start, low, high):
        if top is None:
            parts = [gat[first + i, pl.ds(start, CHUNK), :].astype(jnp.float32) for i in range(2)]
        else:
            parts = [
                jnp.concatenate(
                    [
                        gat[first + i, pl.ds(top, HALO), :],
                        gat[first + i, pl.ds(start, CHUNK - HALO), :],
                    ],
                    axis=0,
                ).astype(jnp.float32)
                for i in range(2)
            ]
        turned = [pltpu.roll(p, 64, 1) for p in parts]
        to[low] = jnp.where(left, parts[0], turned[1]).astype(jnp.bfloat16)
        to[high] = jnp.where(left, turned[0], parts[1]).astype(jnp.bfloat16)

    def unfold_prefix(to, first):
        def one(a, carry):
            for k in range(pk):
                top = None if k else pl.multiple_of(a * HALO, HALO)
                start = tops + a * long_p + max(k * CHUNK - HALO, 0)
                start = pl.multiple_of(start, HALO)
                unfold(to, first, top, start, a * pk + k, (a + seqs // 2) * pk + k)
            return carry

        lax.fori_loop(0, seqs // 2, one, 0)

    def unfold_option(to, first):
        def one(a, carry):
            for k in range(ok):
                top = None if k else pl.multiple_of((seqs // 2 + a) * HALO, HALO)
                start = start_o + a * long_o + max(k * CHUNK - HALO, 0)
                start = pl.multiple_of(start, HALO)
                low = pchunks + a * ok + k
                unfold(to, first, top, start, low, low + opts // 2 * ok)
            return carry

        lax.fori_loop(0, opts // 2, one, 0)

    def score(j, carry):
        raw_scores = dot(cu[j], bu[j], ((1,), (1,)))
        scores[j] = jnp.where(lower, raw_scores, 0.0).astype(jnp.bfloat16)
        return carry

    bc_copy(0, 0, near_slot, near).wait_recv()
    bc_copy(0, 1, far_slot, far).wait_recv()
    bc_copy(0, 2, cross_slot, cross).wait_recv()
    bc_copy(1, 0, near_slot, near).wait_recv()
    bc_copy(1, 2, cross_slot, near).wait_recv()
    unfold_prefix(bu, 0)

    def owner_copy(d, side, s, slot):
        return ctx_copy(
            states.at[slot, side, s], ow_send.at[0], ow_recv.at[d - 1, side], d
        )

    def state_copy(d, side, s, slot):
        return ctx_copy(
            states.at[slot, side, s], st_send.at[d - 1], st_recv.at[d - 1, side], d
        )

    for d in range(1, 5):
        s = lax.rem(c + d, 4)
        state = jnp.zeros((NS, channels), jnp.float32)
        for k in range(pk):
            j = s * pk + k
            if k > 0:
                part[s * (pk - 1) + k - 1] = state
            grown = dot(bu[j], xs[j], ((0,), (0,)))
            state = rows[j, 0:1, :] * state + rows[j, 1:2, :] * grown
        for side in range(2):
            states[c, side, s] = state[:, side * half : (side + 1) * half].astype(jnp.bfloat16)
            if d < 4:
                owner_copy(d, side, s, c).start()

    for side in range(2):
        for d in range(1, 4):

            @pl.when(c + d < 4)
            def _():
                for n in range(3):
                    state_copy(d, side, lax.rem(c + d + 1 + n, 4), c).start()

    bc_copy(2, 1, far_slot, far).wait_recv()
    bc_copy(2, 2, far_slot, near).start()
    lax.fori_loop(0, opts * ok, option_conv, 0)
    bc_copy(2, 0, near_slot, near).wait_recv()
    bc_copy(2, 2, cross_slot, near).wait_recv()
    unfold_option(bu, 0)
    unfold_option(cu, 2)
    unfold_prefix(cu, 2)
    lax.fori_loop(0, chunks, score, 0)

    skip = sg[...]
    skip = dot(
        jnp.concatenate(
            [
                skip.astype(jnp.bfloat16).astype(jnp.float32),
                skip - skip.astype(jnp.bfloat16).astype(jnp.float32),
                jnp.zeros((6, 8), jnp.float32),
            ],
            axis=0,
        ),
        (
            lax.broadcasted_iota(jnp.int32, (8, channels), 0)
            == lax.div(lax.broadcasted_iota(jnp.int32, (8, channels), 1), per_head)
        ).astype(jnp.float32),
    )
    skip = skip[0:1] + skip[1:2]

    def output(j, lo, state, x, gate):
        at = slice(lo, lo + half)
        entering = (state * rows[j, 2:3, at]).astype(jnp.bfloat16)
        y = dot(scores[j], xs[j, :, at]) + dot(cu[j], entering)
        y = ee[j, :, at] * y + skip[:, at] * x.astype(jnp.float32)
        return y * silu(gate.astype(jnp.float32))

    pr, orr = tokens // nh, olen // nh

    def swap_copy(kind, side, to):
        packed, out = ((pack_o, out_o), (pack_p, out_p))[kind]
        return pltpu.make_async_remote_copy(
            src_ref=packed.at[side, to], dst_ref=out.at[side, h],
            send_sem=swap_send.at[kind, side], recv_sem=swap_recv.at[kind, side],
            device_id=(c, to), device_id_type=MESH,
        )

    def own_copy(kind, side):
        packed, out = ((pack_o, out_o), (pack_p, out_p))[kind]
        return pltpu.make_async_copy(packed.at[side, h], out.at[side, h], own_sem.at[kind, side])

    def send_all(kind, side):
        def send(i, carry):
            swap_copy(kind, side, partner(i)).start()
            return carry

        own_copy(kind, side).start()
        lax.fori_loop(1, nh, send, 0)

    def finish(kind, side):
        packed, out = ((pack_o, out_o), (pack_p, out_p))[kind]
        others = pl.ds(0, nh - 1)
        every = pltpu.make_async_remote_copy(
            src_ref=packed.at[side, others], dst_ref=out.at[side, others],
            send_sem=swap_send.at[kind, side], recv_sem=swap_recv.at[kind, side],
            device_id=(c, near), device_id_type=MESH,
        )
        own_copy(kind, side).wait()
        every.wait_send()
        every.wait_recv()

    for d in range(1, 4):
        dec_copy(d, lax.rem(c + 4 - d, 4)).wait_recv()
    loads[2].wait()
    loads[3].wait()
    for side in range(2):
        lo = side * half
        at = slice(lo, lo + half)
        for d in range(1, 4):
            owner_copy(d, side, c, lax.rem(c + 4 - d, 4)).wait_recv()
        final = jnp.zeros((NS, half), jnp.float32)
        for i in range(4):
            final = final * dec[i, pl.ds(c, 1), at] + states[i, side, c].astype(jnp.float32)

        def option_out(o, carry, side=side, lo=lo, at=at, final=final):
            state = final
            for k in range(ok):
                j = pchunks + o * ok + k
                if k > 0:
                    grown = dot(bu[j - 1], xs[j - 1, :, at], ((0,), (0,)))
                    state = rows[j - 1, 0:1, at] * state + rows[j - 1, 1:2, at] * grown
                p = k * CHUNK
                m = output(
                    j, lo, state, xpado[o, HALO + p : HALO + p + CHUNK, at], go[o, p : p + CHUNK, at]
                )
                some = CHUNK // orr
                ybufo[k * some : (k + 1) * some, pl.ds(pl.multiple_of(o * orr, 8), orr), :] = (
                    m.reshape(some, orr, half)
                )
            return carry

        lax.fori_loop(0, opts, option_out, 0)
        for i in range(nh):
            pack_o[side, i] = ybufo[i].astype(jnp.bfloat16)
        send_all(0, side)

    for side in range(2):
        lo = side * half
        at = slice(lo, lo + half)
        for d in range(1, 4):

            @pl.when(c >= d)
            def _():
                ref = states.at[lax.rem(c + 4 - d, 4), side, pl.ds(0, 3)]
                ctx_copy(ref, st_send.at[d - 1], st_recv.at[d - 1, side], d).wait_recv()

        def prefix_out(s, carry, side=side, lo=lo, at=at):
            state = jnp.zeros((NS, half), jnp.float32)
            for i in range(3):
                step = state * dec[i, pl.ds(s, 1), at] + states[i, side, s].astype(jnp.float32)
                state = jnp.where(i < c, step, state)
            factor = jnp.ones((1, half), jnp.float32)
            for k in range(pk):
                j = s * pk + k
                now = state if k == 0 else part[s * (pk - 1) + k - 1, :, at] + state * factor
                p = k * CHUNK
                m = output(
                    j, lo, now, xpad[s, HALO + p : HALO + p + CHUNK, at], gp[s, p : p + CHUNK, at]
                )
                for n in range(half // 128):
                    ybuf[n, pl.ds(seqs * p + s, CHUNK, seqs), :] = m[:, n * 128 : (n + 1) * 128]
                factor = factor * rows[j, 0:1, at]
            return carry

        lax.fori_loop(0, seqs, prefix_out, 0)

        def pack(i, carry, side=side):
            start = pl.multiple_of(i * seqs * pr, 16)
            for n in range(half // 128):
                pack_p[side, i, :, n * 128 : (n + 1) * 128] = ybuf[
                    n, pl.ds(start, seqs * pr), :
                ].astype(jnp.bfloat16)
            return carry

        lax.fori_loop(0, nh, pack, 0)
        send_all(1, side)

    ctx_copy(rim.at[pl.ds(0, 3)], rim_send.at[0], rim_recv.at[0], 1).wait_send()
    ctx_copy(dec.at[pl.ds(0, 3)], dec_send.at[0], dec_recv.at[0], 1).wait_send()
    some = states.at[0, :, pl.ds(0, 3)]
    ctx_copy(some, ow_send.at[0], ow_recv.at[0, 0], 1).wait_send()
    for d in range(1, 4):

        @pl.when(c + d < 4)
        def _():
            ctx_copy(some, st_send.at[d - 1], st_recv.at[d - 1, 0], 1).wait_send()

    some = gat.at[pl.ds(0, 3)]
    pltpu.make_async_remote_copy(
        src_ref=some, dst_ref=some, send_sem=bc_send.at[0], recv_sem=bc_recv.at[0, 0],
        device_id=(c, near), device_id_type=MESH,
    ).wait_send()
    for kind in range(2):
        for side in range(2):
            finish(kind, side)


def norm_kernel(
    seqs, pr, opts, orr, length, values_p, values_o, gain, prefix_out, option_out,
    buf_p, buf_o, res_p, res_o, sems, out_sems,
):
    h = lax.axis_index("head")
    half = values_p.shape[3]
    groups = values_p.shape[1] // 4
    width = 8 * half
    place = lax.broadcasted_iota(jnp.int32, (orr, 1), 0) + h * orr
    keeps = [(place < length[o]).astype(jnp.float32) for o in range(opts)]

    def fetch(group):
        at = pl.ds(group * 4, 4)
        return [
            pltpu.make_async_copy(values.at[:, at], buf.at[:, at], sems.at[n, group])
            for n, (values, buf) in enumerate(((values_p, buf_p), (values_o, buf_o)))
        ]

    def store(group):
        at = pl.ds(group * width, width)
        return [
            pltpu.make_async_copy(res.at[:, :, at], out.at[:, :, at], out_sems.at[n, group])
            for n, (res, out) in enumerate(((res_p, prefix_out), (res_o, option_out)))
        ]

    for group in range(groups):
        for copy in fetch(group):
            copy.start()

    def scale(buf, group):
        squares = None
        for side in range(2):
            for i in range(4):
                block = buf[side, group * 4 + i].astype(jnp.float32)
                squares = block * block if squares is None else squares + block * block
        total = jnp.sum(squares, axis=1, keepdims=True)
        return lax.rsqrt(total / (8 * half) + EPSILON)

    for group in range(groups):
        for copy in fetch(group):
            copy.wait()
        scale_p = scale(buf_p, group)
        scale_o = scale(buf_o, group)
        scale_o = jnp.concatenate(
            [scale_o[o * orr : (o + 1) * orr] * keeps[o] for o in range(opts)], axis=0
        )
        for i in range(4):
            for side in range(2):
                lo = (group * 8 + i * 2 + side) * half
                at = slice(lo, lo + half)
                out = buf_p[side, group * 4 + i].astype(jnp.float32) * scale_p * gain[:, at]
                res_p[:, :, at] = out.reshape(pr, seqs, half).astype(jnp.bfloat16)
                out = buf_o[side, group * 4 + i].astype(jnp.float32) * scale_o * gain[:, at]
                res_o[:, :, at] = out.reshape(opts, orr, half).astype(jnp.bfloat16)
        for copy in store(group):
            copy.start()
    for group in range(groups):
        for copy in store(group):
            copy.wait()


def per_device(
    prefix_x,
    prefix_bc,
    prefix_gate,
    prefix_steps,
    x_kernel,
    bc_kernel,
    step_bias,
    log_rate,
    skip_gain,
    norm_gain,
    option_x,
    option_bc,
    option_gate,
    option_steps,
    option_len,
):
    nh = lax.axis_size("head")
    seqs, tokens, channels = prefix_x.shape
    opts, olen = option_x.shape[0], option_x.shape[1]
    chunks = seqs * (tokens // CHUNK) + opts * (olen // CHUNK)
    half_rows = seqs // 2 * tokens + opts // 2 * olen
    half = channels // 2
    pr, orr = tokens // nh, olen // nh
    bf16, f32 = jnp.bfloat16, jnp.float32
    anywhere = pl.BlockSpec(memory_space=pl.ANY)
    vmem = pl.BlockSpec(memory_space=pltpu.VMEM)
    dma = pltpu.SemaphoreType.DMA
    flip = functools.partial(jnp.swapaxes, axis1=1, axis2=2)

    swapped_p, swapped_o = pl.pallas_call(
        functools.partial(mixer_kernel, nh),
        out_shape=[
            jax.ShapeDtypeStruct((2, nh, seqs * pr, half), bf16),
            jax.ShapeDtypeStruct((2, nh, opts * orr, half), bf16),
        ],
        in_specs=[anywhere, vmem, anywhere, vmem, anywhere, vmem, anywhere, vmem] + [vmem] * 5,
        out_specs=[anywhere, anywhere],
        scratch_shapes=[
            pltpu.VMEM((seqs, HALO + tokens, channels), bf16),
            pltpu.VMEM((opts, HALO + olen, channels), bf16),
            pltpu.VMEM((seqs, tokens, channels), bf16),
            pltpu.VMEM((opts, olen, channels), bf16),
            pltpu.VMEM((4, HALO, channels + 128), bf16),
            pltpu.VMEM((4, half_rows, 128), bf16),
            pltpu.VMEM((4, 2, seqs, NS, half), bf16),
            pltpu.VMEM((4, 8, channels), f32),
            pltpu.VMEM((chunks, CHUNK, channels), bf16),
            pltpu.VMEM((chunks, CHUNK, channels), f32),
            pltpu.VMEM((chunks, 8, channels), f32),
            pltpu.VMEM((chunks, CHUNK, NS), bf16),
            pltpu.VMEM((chunks, CHUNK, NS), bf16),
            pltpu.VMEM((chunks, CHUNK, CHUNK), bf16),
            pltpu.VMEM((seqs * (tokens // CHUNK - 1), NS, channels), f32),
            pltpu.VMEM((half // 128, seqs * tokens, 128), f32),
            pltpu.VMEM((nh, opts * orr, half), f32),
            pltpu.VMEM((2, nh, seqs * pr, half), bf16),
            pltpu.VMEM((2, nh, opts * orr, half), bf16),
            dma((4,)),
            dma((2, 2)),
            dma((1,)), dma((3,)),
            dma((1,)), dma((3, 3)),
            dma((1,)), dma((3, 2)),
            dma((3,)), dma((3, 2)),
            dma((1,)), dma((3,)),
            dma((2, 2)), dma((2, 2)),
        ],
        compiler_params=pltpu.CompilerParams(
            collective_id=0, has_side_effects=True, vmem_limit_bytes=54 * MIB
        ),
        name="mixer",
    )(
        prefix_x, flip(prefix_bc), prefix_gate, flip(prefix_steps),
        option_x, flip(option_bc), option_gate, flip(option_steps),
        x_kernel, bc_kernel,
        step_bias.reshape(1, -1), log_rate.reshape(1, -1), skip_gain.reshape(1, -1),
    )

    inner = nh * channels
    prefix_out, option_out = pl.pallas_call(
        functools.partial(norm_kernel, seqs, pr, opts, orr),
        in_specs=[pl.BlockSpec(memory_space=pltpu.SMEM), anywhere, anywhere, vmem],
        out_specs=[anywhere, anywhere],
        scratch_shapes=[
            pltpu.VMEM((2, nh, seqs * pr, half), bf16),
            pltpu.VMEM((2, nh, opts * orr, half), bf16),
            pltpu.VMEM((pr, seqs, inner), bf16),
            pltpu.VMEM((opts, orr, inner), bf16),
            dma((2, nh // 4)),
            dma((2, nh // 4)),
        ],
        out_shape=[
            jax.ShapeDtypeStruct((pr, seqs, inner), bf16),
            jax.ShapeDtypeStruct((opts, orr, inner), bf16),
        ],
        compiler_params=pltpu.CompilerParams(vmem_limit_bytes=60 * MIB),
        name="norm",
    )(option_len, swapped_p, swapped_o, norm_gain.reshape(1, -1))
    return jnp.swapaxes(prefix_out, 0, 1), option_out


def solution(mesh):
    in_specs = (
        P(None, "ctx", "head"),
        P(None, "ctx", "head"),
        P(None, "ctx", "head"),
        P(None, "ctx", "head"),
        P(None, "head"),
        P(None, "head"),
        P("head"),
        P("head"),
        P("head"),
        P(),
        P("ctx", None, "head"),
        P("ctx", None, "head"),
        P("ctx", None, "head"),
        P("ctx", None, "head"),
        P("ctx"),
    )
    out_specs = (P(None, ("ctx", "head"), None), P("ctx", "head", None))
    return jax.shard_map(
        per_device, mesh=mesh, in_specs=in_specs, out_specs=out_specs, check_vma=False
    )
```

```python
import functools

import jax
import jax.numpy as jnp
from jax import lax
from jax.experimental import pallas as pl
from jax.experimental.pallas import tpu as pltpu
from jax.sharding import PartitionSpec as P

NS = 128
GROUPS = 8
CHUNK = 128
HALO = 16
EPSILON = 1e-05
MESH = pl.DeviceIdType.MESH
MIB = 1 << 20


def silu(v):
    return v / (1.0 + jnp.exp(-v))


def dot(a, b, dims=((1,), (0,)), precision=None):
    return lax.dot_general(
        a, b, (dims, ((), ())), precision=precision, preferred_element_type=jnp.float32
    )


def conv_window(window, taps, rows):
    total = window[HALO - 3 : HALO - 3 + rows] * taps[0:1]
    for k in range(1, 4):
        total = total + window[HALO - 3 + k : HALO - 3 + k + rows] * taps[k : k + 1]
    return silu(total)


def mixer_kernel(
    heads,
    px, pbc, pg, pst, ox, obc, og, ost, xk, bck, sb, lr, sg,
    out_p, out_o,
    xpad, xpado, gp, go, rim, gat, states, dec, xs, ee, rows, bu, cu, scores, part, ybuf, ybufo,
    pack_p, pack_o, rest, gates, factors,
    load_sem, own_sem, rim_send, rim_recv, bc_send, bc_recv, ow_send, ow_recv, st_send, st_recv,
    dec_send, dec_recv, swap_send, swap_recv,
):
    c = lax.axis_index("ctx")
    h = lax.axis_index("head")
    seqs, tokens, channels = px.shape
    opts, olen = ox.shape[0], ox.shape[1]
    nh = heads
    pk, ok = tokens // CHUNK, olen // CHUNK
    pchunks, chunks = seqs * pk, seqs * pk + opts * ok
    cols = pbc.shape[1]
    half = channels // 2
    base = (h // 4) * 4
    r = lax.rem(h, 4)
    near = base + (r + 1 - 2 * lax.rem(r, 2))
    far = base + lax.rem(r + 2, 4)
    far_slot = lax.rem(r + 2, 4)
    near_slot = near - base
    cross = base + lax.rem(near_slot + 2, 4)
    cross_slot = lax.rem(near_slot + 2, 4)
    tops = (seqs // 2 + opts // 2) * HALO
    long_p, long_o = tokens - HALO, olen - HALO
    start_o = tops + seqs // 2 * long_p
    spans = ((0, tops), (tops, seqs // 2 * long_p), (start_o, opts // 2 * long_o))

    loads = [
        pltpu.make_async_copy(px, xpad.at[:, pl.ds(HALO, tokens), :], load_sem.at[0]),
        pltpu.make_async_copy(ox, xpado.at[:, pl.ds(HALO, olen), :], load_sem.at[1]),
        pltpu.make_async_copy(pg, gp, load_sem.at[2]),
        pltpu.make_async_copy(og, go, load_sem.at[3]),
    ]
    for load in loads:
        load.start()

    def partner(i):
        if nh != 32:
            return lax.rem(h + i, nh)
        z, y, k = h // 8, lax.rem(h // 2, 4), lax.rem(h, 2)
        dk, m = lax.rem(i, 2), i // 2
        dz, dy = lax.rem(m, 4), lax.rem(m // 4 + m, 4)
        core = lax.rem(k + dk, 2)
        return lax.rem(z + dz, 4) * 8 + lax.rem(y + dy, 4) * 2 + core

    barrier = pltpu.get_barrier_semaphore()

    def greet(i, carry):
        pl.semaphore_signal(barrier, 1, device_id=(c, lax.rem(h + i, nh)), device_id_type=MESH)
        return carry

    for d in range(1, 4):
        pl.semaphore_signal(barrier, 1, device_id=(lax.rem(c + d, 4), h), device_id_type=MESH)
    lax.fori_loop(1, nh, greet, 0)

    taps = bck[...].astype(jnp.float32)
    taps = jnp.concatenate([taps, taps], axis=1)
    blank = jnp.zeros((HALO, 2 * cols), jnp.float32)

    def pair(ref, a, count):
        both = jnp.concatenate([ref[a], ref[a + count // 2]], axis=0)
        return jnp.transpose(both.astype(jnp.float32))

    heads_p, heads_o, ends = [], [], []
    for a in range(seqs // 2):
        body = pair(pbc, a, seqs)
        heads_p.append(body[0:HALO])
        ends.append(body[tokens - 3 : tokens])
        out = conv_window(body, taps, long_p)
        gat[r, tops + a * long_p : tops + (a + 1) * long_p, :] = out.astype(jnp.bfloat16)
    for a in range(opts // 2):
        body = pair(obc, a, opts)
        heads_o.append(body[0:HALO])
        out = conv_window(body, taps, long_o)
        gat[r, start_o + a * long_o : start_o + (a + 1) * long_o, :] = out.astype(jnp.bfloat16)

    loads[0].wait()
    pad = jnp.zeros((HALO - 3 * seqs, channels), jnp.float32)
    tails = [xpad[s, tokens : tokens + HALO, :].astype(jnp.float32)[HALO - 3 :] for s in range(seqs)]
    rim[c, :, 0:channels] = jnp.concatenate(tails + [pad], axis=0).astype(jnp.bfloat16)
    pad = jnp.zeros((HALO - 3 * len(ends), 2 * cols), jnp.float32)
    rim[c, :, channels : channels + 2 * cols] = jnp.concatenate(ends + [pad], axis=0).astype(
        jnp.bfloat16
    )

    pl.semaphore_wait(barrier, nh + 2)

    def ctx_copy(ref, send, recv, d):
        return pltpu.make_async_remote_copy(
            src_ref=ref, dst_ref=ref, send_sem=send, recv_sem=recv,
            device_id=(lax.rem(c + d, 4), h), device_id_type=MESH,
        )

    def rim_copy(d, slot):
        return ctx_copy(rim.at[slot], rim_send.at[0], rim_recv.at[d - 1], d)

    def bc_copy(part_no, way, slot, target):
        start, count = spans[part_no]
        ref = gat.at[slot, pl.ds(start, count), :]
        return pltpu.make_async_remote_copy(
            src_ref=ref, dst_ref=ref, send_sem=bc_send.at[0],
            recv_sem=bc_recv.at[part_no, way], device_id=(c, target), device_id_type=MESH,
        )

    for d in range(1, 4):
        rim_copy(d, c).start()
    bc_copy(1, 1, r, far).start()
    bc_copy(1, 0, r, near).start()

    same = lax.broadcasted_iota(jnp.int32, (8, 8), 0) == lax.broadcasted_iota(jnp.int32, (8, 8), 1)

    def column(row):
        grown = jnp.where(same, jnp.broadcast_to(row, (8, 8)), 0.0)
        return jnp.concatenate([jnp.sum(grown, axis=1, keepdims=True)] * chunks, axis=0)

    raw = [pst[s, :, k * CHUNK : (k + 1) * CHUNK] for s in range(seqs) for k in range(pk)]
    raw += [ost[o, :, k * CHUNK : (k + 1) * CHUNK] for o in range(opts) for k in range(ok)]
    raw = jnp.concatenate(raw, axis=0) + column(sb[...])
    size = jnp.maximum(raw, 0.0) + jnp.log1p(jnp.exp(-jnp.abs(raw)))
    move = size * column(-jnp.exp(lr[...]))
    across = lax.broadcasted_iota(jnp.int32, (CHUNK, CHUNK), 0)
    along = lax.broadcasted_iota(jnp.int32, (CHUNK, CHUNK), 1)
    lower = across >= along
    cumul = dot(move, (across <= along).astype(jnp.float32), precision=lax.Precision.HIGHEST)
    middle, end = cumul[:, CHUNK // 2 - 1 : CHUNK // 2], cumul[:, CHUNK - 1 : CHUNK]
    place = lax.broadcasted_iota(jnp.int32, cumul.shape, 1)
    few = jnp.where(place == 0, end, jnp.where(place == 1, end - middle, middle))
    wide = [jnp.exp(middle - cumul) * size, jnp.exp(cumul - middle), jnp.exp(few)]
    for n in range(3):
        at = slice(n * CHUNK, (n + 1) * CHUNK)
        high = wide[n].astype(jnp.bfloat16).astype(jnp.float32)
        factors[0, :, at] = high
        factors[1, :, at] = wide[n] - high
    per_head = channels // 8
    pick = lax.broadcasted_iota(jnp.int32, (16, channels), 0)
    pick = lax.rem(pick, 8) == lax.div(lax.broadcasted_iota(jnp.int32, (16, channels), 1), per_head)
    pick = pick.astype(jnp.bfloat16)

    xtaps = xk[...].astype(jnp.float32)

    def convolve(j, window):
        out = conv_window(window, xtaps, CHUNK).astype(jnp.bfloat16)
        at = pl.multiple_of(8 * j, 8)
        both = jnp.concatenate([factors[n, pl.ds(at, 8), :] for n in range(2)], axis=0)
        grown = dot(jnp.transpose(both)[0 : 2 * CHUNK + 8].astype(jnp.bfloat16), pick)
        xs[j] = (out.astype(jnp.float32) * grown[0:CHUNK]).astype(jnp.bfloat16)
        ee[j] = grown[CHUNK : 2 * CHUNK]
        rows[j] = grown[2 * CHUNK : 2 * CHUNK + 8]
        return out

    def prefix_conv(s, k):
        at = k * CHUNK if isinstance(k, int) else pl.multiple_of(k * CHUNK, CHUNK)
        window = xpad[s, pl.ds(at, CHUNK + HALO), :].astype(jnp.float32)
        xpad[s, pl.ds(at + HALO, CHUNK), :] = convolve(s * pk + k, window)

    def option_conv(i, carry):
        o, k = i // ok, ok - 1 - lax.rem(i, ok)
        at = pl.multiple_of(k * CHUNK, CHUNK)
        window = xpado[o, pl.ds(at, CHUNK + HALO), :].astype(jnp.float32)
        xpado[o, pl.ds(at + HALO, CHUNK), :] = convolve(pchunks + o * ok + k, window)
        return carry

    def later_chunks(i, carry):
        prefix_conv(i // (pk - 1), pk - 1 - lax.rem(i, pk - 1))
        return carry

    def first_chunks(s, carry):
        prefix_conv(s, 0)
        return carry

    lax.fori_loop(0, seqs * (pk - 1), later_chunks, 0)

    for d in range(1, 4):
        rim_copy(d, lax.rem(c + 4 - d, 4)).wait_recv()
    before = rim[lax.rem(c + 3, 4)].astype(jnp.float32) * (c > 0).astype(jnp.float32)
    last = rim[3].astype(jnp.float32)
    zeros = jnp.zeros((HALO - 3, channels), jnp.float32)
    owner_tail = jnp.zeros((3, channels), jnp.float32)
    owner_bc = jnp.zeros((3, cols), jnp.float32)
    for s in range(seqs):
        mine = (c == s).astype(jnp.float32)
        tail = before[3 * s : 3 * s + 3, 0:channels]
        xpad[s, 0:HALO, :] = jnp.concatenate([zeros, tail], axis=0).astype(jnp.bfloat16)
        owner_tail = owner_tail + last[3 * s : 3 * s + 3, 0:channels] * mine
        a, side = s % (seqs // 2), channels + cols * (s // (seqs // 2))
        owner_bc = owner_bc + last[3 * a : 3 * a + 3, side : side + cols] * mine
    loads[1].wait()
    for o in range(opts):
        xpado[o, 0:HALO, :] = jnp.concatenate([zeros, owner_tail], axis=0).astype(jnp.bfloat16)
    zeros = jnp.zeros((HALO - 3, 2 * cols), jnp.float32)
    for a in range(seqs // 2):
        tail = before[3 * a : 3 * a + 3, channels : channels + 2 * cols]
        window = jnp.concatenate([zeros, tail, heads_p[a]], axis=0)
        gat[r, a * HALO : (a + 1) * HALO, :] = conv_window(window, taps, HALO).astype(jnp.bfloat16)
    tail = jnp.concatenate([owner_bc, owner_bc], axis=1)
    for a in range(opts // 2):
        at = (seqs // 2 + a) * HALO
        window = jnp.concatenate([zeros, tail, heads_o[a]], axis=0)
        gat[r, at : at + HALO, :] = conv_window(window, taps, HALO).astype(jnp.bfloat16)
    bc_copy(0, 1, r, far).start()
    bc_copy(0, 2, r, cross).start()
    bc_copy(0, 0, r, near).start()

    def from_far():
        bc_copy(1, 1, far_slot, far).wait_recv()
        bc_copy(1, 2, far_slot, near).start()

    def from_far_side():
        bc_copy(0, 1, far_slot, far).wait_recv()
        bc_copy(0, 2, cross_slot, cross).wait_recv()
        bc_copy(1, 2, cross_slot, near).wait_recv()

    def from_near():
        bc_copy(0, 0, near_slot, near).wait_recv()
        bc_copy(1, 0, near_slot, near).wait_recv()

    has_b = r < 2
    pl.when(jnp.logical_not(has_b))(from_far)

    lax.fori_loop(0, seqs, first_chunks, 0)

    for s in range(seqs):
        total = rows[s * pk, 0:1, :]
        for k in range(1, pk):
            total = total * rows[s * pk + k, 0:1, :]
        dec[c, s : s + 1, :] = total

    def dec_copy(d, slot):
        return ctx_copy(dec.at[slot], dec_send.at[0], dec_recv.at[d - 1], d)

    for d in range(1, 4):
        dec_copy(d, c).start()

    left = lax.broadcasted_iota(jnp.int32, (CHUNK, 128), 1) < 64

    def unfold(to, first, top, start, low, high):
        if top is None:
            parts = [gat[first + i, pl.ds(start, CHUNK), :].astype(jnp.float32) for i in range(2)]
        else:
            parts = [
                jnp.concatenate(
                    [
                        gat[first + i, pl.ds(top, HALO), :],
                        gat[first + i, pl.ds(start, CHUNK - HALO), :],
                    ],
                    axis=0,
                ).astype(jnp.float32)
                for i in range(2)
            ]
        turned = [pltpu.roll(p, 64, 1) for p in parts]
        to[low] = jnp.where(left, parts[0], turned[1]).astype(jnp.bfloat16)
        to[high] = jnp.where(left, turned[0], parts[1]).astype(jnp.bfloat16)

    def unfold_prefix(to, first):
        def one(a, carry):
            for k in range(pk):
                top = None if k else pl.multiple_of(a * HALO, HALO)
                start = tops + a * long_p + max(k * CHUNK - HALO, 0)
                start = pl.multiple_of(start, HALO)
                unfold(to, first, top, start, a * pk + k, (a + seqs // 2) * pk + k)
            return carry

        lax.fori_loop(0, seqs // 2, one, 0)

    def unfold_option(to, first):
        def one(a, carry):
            for k in range(ok):
                top = None if k else pl.multiple_of((seqs // 2 + a) * HALO, HALO)
                start = start_o + a * long_o + max(k * CHUNK - HALO, 0)
                start = pl.multiple_of(start, HALO)
                low = pchunks + a * ok + k
                unfold(to, first, top, start, low, low + opts // 2 * ok)
            return carry

        lax.fori_loop(0, opts // 2, one, 0)

    def score(j, carry):
        raw_scores = dot(cu[j], bu[j], ((1,), (1,)))
        scores[j] = jnp.where(lower, raw_scores, 0.0).astype(jnp.bfloat16)
        return carry

    pl.when(has_b)(from_near)
    pl.when(jnp.logical_not(has_b))(from_far_side)
    unfold_prefix(bu, 0)
    bc_copy(2, 1, r, far).start()
    bc_copy(2, 0, r, near).start()

    def owner_copy(d, side, s, slot):
        return ctx_copy(
            states.at[slot, side, s], ow_send.at[0], ow_recv.at[d - 1, side], d
        )

    def state_copy(d, side, s, slot):
        return ctx_copy(
            states.at[slot, side, s], st_send.at[d - 1], st_recv.at[d - 1, side], d
        )

    for d in range(1, 5):
        s = lax.rem(c + d, 4)
        state = jnp.zeros((NS, channels), jnp.float32)
        for k in range(pk):
            j = s * pk + k
            if k > 0:
                part[s * (pk - 1) + k - 1] = state
            grown = dot(bu[j], xs[j], ((0,), (0,)))
            state = rows[j, 0:1, :] * state + rows[j, 1:2, :] * grown
        for side in range(2):
            states[c, side, s] = state[:, side * half : (side + 1) * half].astype(jnp.bfloat16)
        if d < 4:
            owner_copy(d, 0, s, c).start()
    for d in range(1, 4):
        owner_copy(d, 1, lax.rem(c + d, 4), c).start()

    for side in range(2):
        for d in range(1, 4):

            @pl.when(c + d < 4)
            def _():
                for n in range(3):
                    state_copy(d, side, lax.rem(c + d + 1 + n, 4), c).start()

    pl.when(has_b)(from_far)
    lax.fori_loop(0, opts * ok, option_conv, 0)
    bc_copy(2, 1, far_slot, far).wait_recv()
    bc_copy(2, 2, far_slot, near).start()
    pl.when(has_b)(from_far_side)
    pl.when(jnp.logical_not(has_b))(from_near)
    bc_copy(2, 0, near_slot, near).wait_recv()
    bc_copy(2, 2, cross_slot, near).wait_recv()
    unfold_option(bu, 0)
    unfold_option(cu, 2)
    lax.fori_loop(pchunks, chunks, score, 0)

    skip = sg[...]
    skip = dot(
        jnp.concatenate(
            [
                skip.astype(jnp.bfloat16).astype(jnp.float32),
                skip - skip.astype(jnp.bfloat16).astype(jnp.float32),
                jnp.zeros((6, 8), jnp.float32),
            ],
            axis=0,
        ),
        (
            lax.broadcasted_iota(jnp.int32, (8, channels), 0)
            == lax.div(lax.broadcasted_iota(jnp.int32, (8, channels), 1), per_head)
        ).astype(jnp.float32),
    )
    skip = skip[0:1] + skip[1:2]

    loads[3].wait()

    def option_rest(at):
        def one(i, carry):
            o, k = i // ok, lax.rem(i, ok)
            p = pl.multiple_of(k * CHUNK, CHUNK)
            j = pchunks + i
            x = xpado[o, pl.ds(p + HALO, CHUNK), at].astype(jnp.float32)
            rest[i] = ee[j, :, at] * dot(scores[j], xs[j, :, at]) + skip[:, at] * x
            gates[i] = silu(go[o, pl.ds(p, CHUNK), at].astype(jnp.float32))
            return carry

        lax.fori_loop(0, opts * ok, one, 0)

    def output(j, lo, state, x, gate):
        at = slice(lo, lo + half)
        entering = (state * rows[j, 2:3, at]).astype(jnp.bfloat16)
        y = dot(scores[j], xs[j, :, at]) + dot(cu[j], entering)
        y = ee[j, :, at] * y + skip[:, at] * x.astype(jnp.float32)
        return y * silu(gate.astype(jnp.float32))

    pr, orr = tokens // nh, olen // nh

    def swap_copy(kind, side, to):
        packed, out = ((pack_o, out_o), (pack_p, out_p))[kind]
        return pltpu.make_async_remote_copy(
            src_ref=packed.at[side, to], dst_ref=out.at[side, h],
            send_sem=swap_send.at[kind, side], recv_sem=swap_recv.at[kind, side],
            device_id=(c, to), device_id_type=MESH,
        )

    def own_copy(kind, side):
        packed, out = ((pack_o, out_o), (pack_p, out_p))[kind]
        return pltpu.make_async_copy(packed.at[side, h], out.at[side, h], own_sem.at[kind, side])

    def send_all(kind, side):
        def send(i, carry):
            swap_copy(kind, side, partner(i)).start()
            return carry

        own_copy(kind, side).start()
        lax.fori_loop(1, nh, send, 0)

    def finish(kind, side):
        packed, out = ((pack_o, out_o), (pack_p, out_p))[kind]
        others = pl.ds(0, nh - 1)
        every = pltpu.make_async_remote_copy(
            src_ref=packed.at[side, others], dst_ref=out.at[side, others],
            send_sem=swap_send.at[kind, side], recv_sem=swap_recv.at[kind, side],
            device_id=(c, near), device_id_type=MESH,
        )
        own_copy(kind, side).wait()
        every.wait_send()
        every.wait_recv()

    for d in range(1, 4):
        dec_copy(d, lax.rem(c + 4 - d, 4)).wait_recv()
    loads[2].wait()
    for side in range(2):
        lo = side * half
        at = slice(lo, lo + half)
        option_rest(at)
        for d in range(1, 4):
            owner_copy(d, side, c, lax.rem(c + 4 - d, 4)).wait_recv()
        final = jnp.zeros((NS, half), jnp.float32)
        for i in range(4):
            final = final * dec[i, pl.ds(c, 1), at] + states[i, side, c].astype(jnp.float32)

        def option_out(o, carry, side=side, lo=lo, at=at, final=final):
            state = final
            for k in range(ok):
                j = pchunks + o * ok + k
                if k > 0:
                    grown = dot(bu[j - 1], xs[j - 1, :, at], ((0,), (0,)))
                    state = rows[j - 1, 0:1, at] * state + rows[j - 1, 1:2, at] * grown
                p = k * CHUNK
                entering = (state * rows[j, 2:3, at]).astype(jnp.bfloat16)
                y = rest[o * ok + k] + ee[j, :, at] * dot(cu[j], entering)
                m = y * gates[o * ok + k]
                some = CHUNK // orr
                ybufo[k * some : (k + 1) * some, pl.ds(pl.multiple_of(o * orr, 8), orr), :] = (
                    m.reshape(some, orr, half)
                )
            return carry

        lax.fori_loop(0, opts, option_out, 0)
        for i in range(nh):
            pack_o[side, i] = ybufo[i].astype(jnp.bfloat16)
        send_all(0, side)

    unfold_prefix(cu, 2)
    lax.fori_loop(0, pchunks, score, 0)

    for side in range(2):
        lo = side * half
        at = slice(lo, lo + half)
        for d in range(1, 4):

            @pl.when(c >= d)
            def _():
                ref = states.at[lax.rem(c + 4 - d, 4), side, pl.ds(0, 3)]
                ctx_copy(ref, st_send.at[d - 1], st_recv.at[d - 1, side], d).wait_recv()

        def prefix_out(s, carry, side=side, lo=lo, at=at):
            state = jnp.zeros((NS, half), jnp.float32)
            for i in range(3):
                step = state * dec[i, pl.ds(s, 1), at] + states[i, side, s].astype(jnp.float32)
                state = jnp.where(i < c, step, state)
            factor = jnp.ones((1, half), jnp.float32)
            for k in range(pk):
                j = s * pk + k
                now = state if k == 0 else part[s * (pk - 1) + k - 1, :, at] + state * factor
                p = k * CHUNK
                m = output(
                    j, lo, now, xpad[s, HALO + p : HALO + p + CHUNK, at], gp[s, p : p + CHUNK, at]
                )
                for n in range(half // 128):
                    ybuf[n, pl.ds(seqs * p + s, CHUNK, seqs), :] = m[:, n * 128 : (n + 1) * 128]
                factor = factor * rows[j, 0:1, at]
            return carry

        lax.fori_loop(0, seqs, prefix_out, 0)

        def pack(i, carry, side=side):
            start = pl.multiple_of(i * seqs * pr, 16)
            for n in range(half // 128):
                pack_p[side, i, :, n * 128 : (n + 1) * 128] = ybuf[
                    n, pl.ds(start, seqs * pr), :
                ].astype(jnp.bfloat16)
            return carry

        lax.fori_loop(0, nh, pack, 0)
        send_all(1, side)

    ctx_copy(rim.at[pl.ds(0, 3)], rim_send.at[0], rim_recv.at[0], 1).wait_send()
    ctx_copy(dec.at[pl.ds(0, 3)], dec_send.at[0], dec_recv.at[0], 1).wait_send()
    some = states.at[0, :, pl.ds(0, 3)]
    ctx_copy(some, ow_send.at[0], ow_recv.at[0, 0], 1).wait_send()
    for d in range(1, 4):

        @pl.when(c + d < 4)
        def _():
            ctx_copy(some, st_send.at[d - 1], st_recv.at[d - 1, 0], 1).wait_send()

    some = gat.at[pl.ds(0, 3)]
    pltpu.make_async_remote_copy(
        src_ref=some, dst_ref=some, send_sem=bc_send.at[0], recv_sem=bc_recv.at[0, 0],
        device_id=(c, near), device_id_type=MESH,
    ).wait_send()
    for kind in range(2):
        for side in range(2):
            finish(kind, side)


def norm_kernel(
    seqs, pr, opts, orr, length, values_p, values_o, gain, prefix_out, option_out,
    buf_p, buf_o, res_p, res_o, sems, out_sems,
):
    h = lax.axis_index("head")
    half = values_p.shape[3]
    groups = values_p.shape[1] // 4
    width = 8 * half
    place = lax.broadcasted_iota(jnp.int32, (orr, 1), 0) + h * orr
    keeps = [(place < length[o]).astype(jnp.float32) for o in range(opts)]

    def fetch(group):
        at = pl.ds(group * 4, 4)
        return [
            pltpu.make_async_copy(values.at[:, at], buf.at[:, at], sems.at[n, group])
            for n, (values, buf) in enumerate(((values_p, buf_p), (values_o, buf_o)))
        ]

    def store(group):
        at = pl.ds(group * width, width)
        return [
            pltpu.make_async_copy(res.at[:, :, at], out.at[:, :, at], out_sems.at[n, group])
            for n, (res, out) in enumerate(((res_p, prefix_out), (res_o, option_out)))
        ]

    for group in range(groups):
        for copy in fetch(group):
            copy.start()

    def scale(buf, group):
        squares = None
        for side in range(2):
            for i in range(4):
                block = buf[side, group * 4 + i].astype(jnp.float32)
                squares = block * block if squares is None else squares + block * block
        total = jnp.sum(squares, axis=1, keepdims=True)
        return lax.rsqrt(total / (8 * half) + EPSILON)

    for group in range(groups):
        for copy in fetch(group):
            copy.wait()
        scale_p = scale(buf_p, group)
        scale_o = scale(buf_o, group)
        scale_o = jnp.concatenate(
            [scale_o[o * orr : (o + 1) * orr] * keeps[o] for o in range(opts)], axis=0
        )
        for i in range(4):
            for side in range(2):
                lo = (group * 8 + i * 2 + side) * half
                at = slice(lo, lo + half)
                out = buf_p[side, group * 4 + i].astype(jnp.float32) * scale_p * gain[:, at]
                res_p[:, :, at] = out.reshape(pr, seqs, half).astype(jnp.bfloat16)
                out = buf_o[side, group * 4 + i].astype(jnp.float32) * scale_o * gain[:, at]
                res_o[:, :, at] = out.reshape(opts, orr, half).astype(jnp.bfloat16)
        for copy in store(group):
            copy.start()
    for group in range(groups):
        for copy in store(group):
            copy.wait()


def per_device(
    prefix_x,
    prefix_bc,
    prefix_gate,
    prefix_steps,
    x_kernel,
    bc_kernel,
    step_bias,
    log_rate,
    skip_gain,
    norm_gain,
    option_x,
    option_bc,
    option_gate,
    option_steps,
    option_len,
):
    nh = lax.axis_size("head")
    seqs, tokens, channels = prefix_x.shape
    opts, olen = option_x.shape[0], option_x.shape[1]
    chunks = seqs * (tokens // CHUNK) + opts * (olen // CHUNK)
    half_rows = seqs // 2 * tokens + opts // 2 * olen
    half = channels // 2
    pr, orr = tokens // nh, olen // nh
    bf16, f32 = jnp.bfloat16, jnp.float32
    anywhere = pl.BlockSpec(memory_space=pl.ANY)
    vmem = pl.BlockSpec(memory_space=pltpu.VMEM)
    dma = pltpu.SemaphoreType.DMA
    flip = functools.partial(jnp.swapaxes, axis1=1, axis2=2)

    swapped_p, swapped_o = pl.pallas_call(
        functools.partial(mixer_kernel, nh),
        out_shape=[
            jax.ShapeDtypeStruct((2, nh, seqs * pr, half), bf16),
            jax.ShapeDtypeStruct((2, nh, opts * orr, half), bf16),
        ],
        in_specs=[anywhere, vmem, anywhere, vmem, anywhere, vmem, anywhere, vmem] + [vmem] * 5,
        out_specs=[anywhere, anywhere],
        scratch_shapes=[
            pltpu.VMEM((seqs, HALO + tokens, channels), bf16),
            pltpu.VMEM((opts, HALO + olen, channels), bf16),
            pltpu.VMEM((seqs, tokens, channels), bf16),
            pltpu.VMEM((opts, olen, channels), bf16),
            pltpu.VMEM((4, HALO, channels + 128), bf16),
            pltpu.VMEM((4, half_rows, 128), bf16),
            pltpu.VMEM((4, 2, seqs, NS, half), bf16),
            pltpu.VMEM((4, 8, channels), f32),
            pltpu.VMEM((chunks, CHUNK, channels), bf16),
            pltpu.VMEM((chunks, CHUNK, channels), f32),
            pltpu.VMEM((chunks, 8, channels), f32),
            pltpu.VMEM((chunks, CHUNK, NS), bf16),
            pltpu.VMEM((chunks, CHUNK, NS), bf16),
            pltpu.VMEM((chunks, CHUNK, CHUNK), bf16),
            pltpu.VMEM((seqs * (tokens // CHUNK - 1), NS, channels), f32),
            pltpu.VMEM((half // 128, seqs * tokens, 128), f32),
            pltpu.VMEM((nh, opts * orr, half), f32),
            pltpu.VMEM((2, nh, seqs * pr, half), bf16),
            pltpu.VMEM((2, nh, opts * orr, half), bf16),
            pltpu.VMEM((opts * olen // CHUNK, CHUNK, half), f32),
            pltpu.VMEM((opts * olen // CHUNK, CHUNK, half), f32),
            pltpu.VMEM((2, 8 * chunks, 3 * CHUNK), f32),
            dma((4,)),
            dma((2, 2)),
            dma((1,)), dma((3,)),
            dma((1,)), dma((3, 3)),
            dma((1,)), dma((3, 2)),
            dma((3,)), dma((3, 2)),
            dma((1,)), dma((3,)),
            dma((2, 2)), dma((2, 2)),
        ],
        compiler_params=pltpu.CompilerParams(
            collective_id=0, has_side_effects=True, vmem_limit_bytes=54 * MIB
        ),
        name="mixer",
    )(
        prefix_x, flip(prefix_bc), prefix_gate, flip(prefix_steps),
        option_x, flip(option_bc), option_gate, flip(option_steps),
        x_kernel, bc_kernel,
        step_bias.reshape(1, -1), log_rate.reshape(1, -1), skip_gain.reshape(1, -1),
    )

    inner = nh * channels
    prefix_out, option_out = pl.pallas_call(
        functools.partial(norm_kernel, seqs, pr, opts, orr),
        in_specs=[pl.BlockSpec(memory_space=pltpu.SMEM), anywhere, anywhere, vmem],
        out_specs=[anywhere, anywhere],
        scratch_shapes=[
            pltpu.VMEM((2, nh, seqs * pr, half), bf16),
            pltpu.VMEM((2, nh, opts * orr, half), bf16),
            pltpu.VMEM((pr, seqs, inner), bf16),
            pltpu.VMEM((opts, orr, inner), bf16),
            dma((2, nh // 4)),
            dma((2, nh // 4)),
        ],
        out_shape=[
            jax.ShapeDtypeStruct((pr, seqs, inner), bf16),
            jax.ShapeDtypeStruct((opts, orr, inner), bf16),
        ],
        compiler_params=pltpu.CompilerParams(vmem_limit_bytes=60 * MIB),
        name="norm",
    )(option_len, swapped_p, swapped_o, norm_gain.reshape(1, -1))
    return jnp.swapaxes(prefix_out, 0, 1), option_out


def solution(mesh):
    in_specs = (
        P(None, "ctx", "head"),
        P(None, "ctx", "head"),
        P(None, "ctx", "head"),
        P(None, "ctx", "head"),
        P(None, "head"),
        P(None, "head"),
        P("head"),
        P("head"),
        P("head"),
        P(),
        P("ctx", None, "head"),
        P("ctx", None, "head"),
        P("ctx", None, "head"),
        P("ctx", None, "head"),
        P("ctx"),
    )
    out_specs = (P(None, ("ctx", "head"), None), P("ctx", "head", None))
    return jax.shard_map(
        per_device, mesh=mesh, in_specs=in_specs, out_specs=out_specs, check_vma=False
    )
```

```python
import functools

import jax
import jax.numpy as jnp
from jax import lax
from jax.experimental import pallas as pl
from jax.experimental.pallas import tpu as pltpu
from jax.sharding import PartitionSpec as P

NS = 128
GROUPS = 8
CHUNK = 128
HALO = 16
EPSILON = 1e-05
MESH = pl.DeviceIdType.MESH
MIB = 1 << 20


def silu(v):
    return v / (1.0 + jnp.exp(-v))


def dot(a, b, dims=((1,), (0,)), precision=None):
    return lax.dot_general(
        a, b, (dims, ((), ())), precision=precision, preferred_element_type=jnp.float32
    )


def conv_window(window, taps, rows):
    total = window[HALO - 3 : HALO - 3 + rows] * taps[0:1]
    for k in range(1, 4):
        total = total + window[HALO - 3 + k : HALO - 3 + k + rows] * taps[k : k + 1]
    return silu(total)


def mixer_kernel(
    heads,
    px, pbc, pg, pst, ox, obc, og, ost, xk, bck, sb, lr, sg, gain, length,
    out_p, out_o,
    xpad, xpado, gp, go, rim, gat, states, dec, xs, ee, rows, bu, cu, scores, part, ybuf, ybufo,
    pack_p, pack_o, rest, gates, factors, got_o, res_o,
    load_sem, own_sem, rim_send, rim_recv, bc_send, bc_recv, ow_send, ow_recv, st_send, st_recv,
    dec_send, dec_recv, swap_send, swap_recv,
):
    c = lax.axis_index("ctx")
    h = lax.axis_index("head")
    seqs, tokens, channels = px.shape
    opts, olen = ox.shape[0], ox.shape[1]
    nh = heads
    pk, ok = tokens // CHUNK, olen // CHUNK
    pchunks, chunks = seqs * pk, seqs * pk + opts * ok
    cols = pbc.shape[1]
    half = channels // 2
    base = (h // 4) * 4
    r = lax.rem(h, 4)
    near = base + (r + 1 - 2 * lax.rem(r, 2))
    far = base + lax.rem(r + 2, 4)
    far_slot = lax.rem(r + 2, 4)
    near_slot = near - base
    cross = base + lax.rem(near_slot + 2, 4)
    cross_slot = lax.rem(near_slot + 2, 4)
    tops = (seqs // 2 + opts // 2) * HALO
    long_p, long_o = tokens - HALO, olen - HALO
    start_o = tops + seqs // 2 * long_p
    spans = ((0, tops), (tops, seqs // 2 * long_p), (start_o, opts // 2 * long_o))

    loads = [
        pltpu.make_async_copy(px, xpad.at[:, pl.ds(HALO, tokens), :], load_sem.at[0]),
        pltpu.make_async_copy(ox, xpado.at[:, pl.ds(HALO, olen), :], load_sem.at[1]),
        pltpu.make_async_copy(pg, gp, load_sem.at[2]),
        pltpu.make_async_copy(og, go, load_sem.at[3]),
    ]
    for load in loads:
        load.start()

    def partner(i):
        if nh != 32:
            return lax.rem(h + i, nh)
        z, y, k = h // 8, lax.rem(h // 2, 4), lax.rem(h, 2)
        dk, m = lax.rem(i, 2), i // 2
        dz, dy = lax.rem(m, 4), lax.rem(m // 4 + m, 4)
        core = lax.rem(k + dk, 2)
        return lax.rem(z + dz, 4) * 8 + lax.rem(y + dy, 4) * 2 + core

    barrier = pltpu.get_barrier_semaphore()

    def greet(i, carry):
        pl.semaphore_signal(barrier, 1, device_id=(c, lax.rem(h + i, nh)), device_id_type=MESH)
        return carry

    for d in range(1, 4):
        pl.semaphore_signal(barrier, 1, device_id=(lax.rem(c + d, 4), h), device_id_type=MESH)
    lax.fori_loop(1, nh, greet, 0)

    taps = bck[...].astype(jnp.float32)
    taps = jnp.concatenate([taps, taps], axis=1)
    blank = jnp.zeros((HALO, 2 * cols), jnp.float32)

    def pair(ref, a, count):
        both = jnp.concatenate([ref[a], ref[a + count // 2]], axis=0)
        return jnp.transpose(both.astype(jnp.float32))

    heads_p, heads_o, ends = [], [], []
    for a in range(seqs // 2):
        body = pair(pbc, a, seqs)
        heads_p.append(body[0:HALO])
        ends.append(body[tokens - 3 : tokens])
        out = conv_window(body, taps, long_p)
        gat[r, tops + a * long_p : tops + (a + 1) * long_p, :] = out.astype(jnp.bfloat16)
    for a in range(opts // 2):
        body = pair(obc, a, opts)
        heads_o.append(body[0:HALO])
        out = conv_window(body, taps, long_o)
        gat[r, start_o + a * long_o : start_o + (a + 1) * long_o, :] = out.astype(jnp.bfloat16)

    loads[0].wait()
    pad = jnp.zeros((HALO - 3 * seqs, channels), jnp.float32)
    tails = [xpad[s, tokens : tokens + HALO, :].astype(jnp.float32)[HALO - 3 :] for s in range(seqs)]
    rim[c, :, 0:channels] = jnp.concatenate(tails + [pad], axis=0).astype(jnp.bfloat16)
    pad = jnp.zeros((HALO - 3 * len(ends), 2 * cols), jnp.float32)
    rim[c, :, channels : channels + 2 * cols] = jnp.concatenate(ends + [pad], axis=0).astype(
        jnp.bfloat16
    )

    pl.semaphore_wait(barrier, nh + 2)

    def ctx_copy(ref, send, recv, d):
        return pltpu.make_async_remote_copy(
            src_ref=ref, dst_ref=ref, send_sem=send, recv_sem=recv,
            device_id=(lax.rem(c + d, 4), h), device_id_type=MESH,
        )

    def rim_copy(d, slot):
        return ctx_copy(rim.at[slot], rim_send.at[0], rim_recv.at[d - 1], d)

    def bc_copy(part_no, way, slot, target):
        start, count = spans[part_no]
        ref = gat.at[slot, pl.ds(start, count), :]
        return pltpu.make_async_remote_copy(
            src_ref=ref, dst_ref=ref, send_sem=bc_send.at[0],
            recv_sem=bc_recv.at[part_no, way], device_id=(c, target), device_id_type=MESH,
        )

    for d in range(1, 4):
        rim_copy(d, c).start()
    bc_copy(1, 1, r, far).start()
    bc_copy(1, 0, r, near).start()

    same = lax.broadcasted_iota(jnp.int32, (8, 8), 0) == lax.broadcasted_iota(jnp.int32, (8, 8), 1)

    def column(row):
        grown = jnp.where(same, jnp.broadcast_to(row, (8, 8)), 0.0)
        return jnp.concatenate([jnp.sum(grown, axis=1, keepdims=True)] * chunks, axis=0)

    raw = [pst[s, :, k * CHUNK : (k + 1) * CHUNK] for s in range(seqs) for k in range(pk)]
    raw += [ost[o, :, k * CHUNK : (k + 1) * CHUNK] for o in range(opts) for k in range(ok)]
    raw = jnp.concatenate(raw, axis=0) + column(sb[...])
    size = jnp.maximum(raw, 0.0) + jnp.log1p(jnp.exp(-jnp.abs(raw)))
    move = size * column(-jnp.exp(lr[...]))
    across = lax.broadcasted_iota(jnp.int32, (CHUNK, CHUNK), 0)
    along = lax.broadcasted_iota(jnp.int32, (CHUNK, CHUNK), 1)
    lower = across >= along
    cumul = dot(move, (across <= along).astype(jnp.float32), precision=lax.Precision.HIGHEST)
    middle, end = cumul[:, CHUNK // 2 - 1 : CHUNK // 2], cumul[:, CHUNK - 1 : CHUNK]
    place = lax.broadcasted_iota(jnp.int32, cumul.shape, 1)
    few = jnp.where(place == 0, end, jnp.where(place == 1, end - middle, middle))
    wide = [jnp.exp(middle - cumul) * size, jnp.exp(cumul - middle), jnp.exp(few)]
    for n in range(3):
        at = slice(n * CHUNK, (n + 1) * CHUNK)
        high = wide[n].astype(jnp.bfloat16).astype(jnp.float32)
        factors[0, :, at] = high
        factors[1, :, at] = wide[n] - high
    per_head = channels // 8
    pick = lax.broadcasted_iota(jnp.int32, (16, channels), 0)
    pick = lax.rem(pick, 8) == lax.div(lax.broadcasted_iota(jnp.int32, (16, channels), 1), per_head)
    pick = pick.astype(jnp.bfloat16)

    xtaps = xk[...].astype(jnp.float32)

    def convolve(j, window):
        out = conv_window(window, xtaps, CHUNK).astype(jnp.bfloat16)
        at = pl.multiple_of(8 * j, 8)
        both = jnp.concatenate([factors[n, pl.ds(at, 8), :] for n in range(2)], axis=0)
        grown = dot(jnp.transpose(both)[0 : 2 * CHUNK + 8].astype(jnp.bfloat16), pick)
        xs[j] = (out.astype(jnp.float32) * grown[0:CHUNK]).astype(jnp.bfloat16)
        ee[j] = grown[CHUNK : 2 * CHUNK]
        rows[j] = grown[2 * CHUNK : 2 * CHUNK + 8]
        return out

    def prefix_conv(s, k):
        at = k * CHUNK if isinstance(k, int) else pl.multiple_of(k * CHUNK, CHUNK)
        window = xpad[s, pl.ds(at, CHUNK + HALO), :].astype(jnp.float32)
        xpad[s, pl.ds(at + HALO, CHUNK), :] = convolve(s * pk + k, window)

    def option_conv(i, carry):
        o, k = i // ok, ok - 1 - lax.rem(i, ok)
        at = pl.multiple_of(k * CHUNK, CHUNK)
        window = xpado[o, pl.ds(at, CHUNK + HALO), :].astype(jnp.float32)
        xpado[o, pl.ds(at + HALO, CHUNK), :] = convolve(pchunks + o * ok + k, window)
        return carry

    def later_chunks(i, carry):
        prefix_conv(i // (pk - 1), pk - 1 - lax.rem(i, pk - 1))
        return carry

    def first_chunks(s, carry):
        prefix_conv(s, 0)
        return carry

    lax.fori_loop(0, seqs * (pk - 1), later_chunks, 0, unroll=2)

    for d in range(1, 4):
        rim_copy(d, lax.rem(c + 4 - d, 4)).wait_recv()
    before = rim[lax.rem(c + 3, 4)].astype(jnp.float32) * (c > 0).astype(jnp.float32)
    last = rim[3].astype(jnp.float32)
    zeros = jnp.zeros((HALO - 3, channels), jnp.float32)
    owner_tail = jnp.zeros((3, channels), jnp.float32)
    owner_bc = jnp.zeros((3, cols), jnp.float32)
    for s in range(seqs):
        mine = (c == s).astype(jnp.float32)
        tail = before[3 * s : 3 * s + 3, 0:channels]
        xpad[s, 0:HALO, :] = jnp.concatenate([zeros, tail], axis=0).astype(jnp.bfloat16)
        owner_tail = owner_tail + last[3 * s : 3 * s + 3, 0:channels] * mine
        a, side = s % (seqs // 2), channels + cols * (s // (seqs // 2))
        owner_bc = owner_bc + last[3 * a : 3 * a + 3, side : side + cols] * mine
    loads[1].wait()
    for o in range(opts):
        xpado[o, 0:HALO, :] = jnp.concatenate([zeros, owner_tail], axis=0).astype(jnp.bfloat16)
    zeros = jnp.zeros((HALO - 3, 2 * cols), jnp.float32)
    for a in range(seqs // 2):
        tail = before[3 * a : 3 * a + 3, channels : channels + 2 * cols]
        window = jnp.concatenate([zeros, tail, heads_p[a]], axis=0)
        gat[r, a * HALO : (a + 1) * HALO, :] = conv_window(window, taps, HALO).astype(jnp.bfloat16)
    tail = jnp.concatenate([owner_bc, owner_bc], axis=1)
    for a in range(opts // 2):
        at = (seqs // 2 + a) * HALO
        window = jnp.concatenate([zeros, tail, heads_o[a]], axis=0)
        gat[r, at : at + HALO, :] = conv_window(window, taps, HALO).astype(jnp.bfloat16)
    bc_copy(0, 1, r, far).start()
    bc_copy(0, 2, r, cross).start()
    bc_copy(0, 0, r, near).start()

    def from_far():
        bc_copy(1, 1, far_slot, far).wait_recv()
        bc_copy(1, 2, far_slot, near).start()

    def from_far_side():
        bc_copy(0, 1, far_slot, far).wait_recv()
        bc_copy(0, 2, cross_slot, cross).wait_recv()
        bc_copy(1, 2, cross_slot, near).wait_recv()

    def from_near():
        bc_copy(0, 0, near_slot, near).wait_recv()
        bc_copy(1, 0, near_slot, near).wait_recv()

    has_b = r < 2
    pl.when(jnp.logical_not(has_b))(from_far)

    lax.fori_loop(0, seqs, first_chunks, 0, unroll=2)

    for s in range(seqs):
        total = rows[s * pk, 0:1, :]
        for k in range(1, pk):
            total = total * rows[s * pk + k, 0:1, :]
        dec[c, s : s + 1, :] = total

    def dec_copy(d, slot):
        return ctx_copy(dec.at[slot], dec_send.at[0], dec_recv.at[d - 1], d)

    for d in range(1, 4):
        dec_copy(d, c).start()

    left = lax.broadcasted_iota(jnp.int32, (CHUNK, 128), 1) < 64

    def unfold(to, first, top, start, low, high):
        if top is None:
            parts = [gat[first + i, pl.ds(start, CHUNK), :].astype(jnp.float32) for i in range(2)]
        else:
            parts = [
                jnp.concatenate(
                    [
                        gat[first + i, pl.ds(top, HALO), :],
                        gat[first + i, pl.ds(start, CHUNK - HALO), :],
                    ],
                    axis=0,
                ).astype(jnp.float32)
                for i in range(2)
            ]
        turned = [pltpu.roll(p, 64, 1) for p in parts]
        to[low] = jnp.where(left, parts[0], turned[1]).astype(jnp.bfloat16)
        to[high] = jnp.where(left, turned[0], parts[1]).astype(jnp.bfloat16)

    def unfold_prefix(to, first):
        def one(a, carry):
            for k in range(pk):
                top = None if k else pl.multiple_of(a * HALO, HALO)
                start = tops + a * long_p + max(k * CHUNK - HALO, 0)
                start = pl.multiple_of(start, HALO)
                unfold(to, first, top, start, a * pk + k, (a + seqs // 2) * pk + k)
            return carry

        lax.fori_loop(0, seqs // 2, one, 0)

    def unfold_option(to, first):
        def one(a, carry):
            for k in range(ok):
                top = None if k else pl.multiple_of((seqs // 2 + a) * HALO, HALO)
                start = start_o + a * long_o + max(k * CHUNK - HALO, 0)
                start = pl.multiple_of(start, HALO)
                low = pchunks + a * ok + k
                unfold(to, first, top, start, low, low + opts // 2 * ok)
            return carry

        lax.fori_loop(0, opts // 2, one, 0)

    def score(j, carry):
        raw_scores = dot(cu[j], bu[j], ((1,), (1,)))
        scores[j] = jnp.where(lower, raw_scores, 0.0).astype(jnp.bfloat16)
        return carry

    pl.when(has_b)(from_near)
    pl.when(jnp.logical_not(has_b))(from_far_side)
    unfold_prefix(bu, 0)
    bc_copy(2, 1, r, far).start()
    bc_copy(2, 0, r, near).start()

    def owner_copy(d, side, s, slot):
        return ctx_copy(
            states.at[slot, side, s], ow_send.at[0], ow_recv.at[d - 1, side], d
        )

    for d in range(1, 5):
        s = lax.rem(c + d, 4)
        state = jnp.zeros((NS, channels), jnp.float32)
        for k in range(pk):
            j = s * pk + k
            if k > 0:
                part[s * (pk - 1) + k - 1] = state
            grown = dot(bu[j], xs[j], ((0,), (0,)))
            state = rows[j, 0:1, :] * state + rows[j, 1:2, :] * grown
        for side in range(2):
            states[c, side, s] = state[:, side * half : (side + 1) * half].astype(jnp.bfloat16)
        if d < 4:
            owner_copy(d, 0, s, c).start()
    for d in range(1, 4):
        owner_copy(d, 1, lax.rem(c + d, 4), c).start()

    pl.when(has_b)(from_far)
    lax.fori_loop(0, opts * ok, option_conv, 0, unroll=2)
    for side in range(2):
        for later in range(1, 4):

            @pl.when(c < later)
            def _():
                d = later - c
                for first, end_ in ((0, later), (later + 1, 4)):
                    if first < end_:
                        ref = states.at[c, side, pl.ds(first, end_ - first)]
                        ctx_copy(ref, st_send.at[d - 1], st_recv.at[d - 1, side], d).start()

    bc_copy(2, 1, far_slot, far).wait_recv()
    bc_copy(2, 2, far_slot, near).start()
    pl.when(has_b)(from_far_side)
    pl.when(jnp.logical_not(has_b))(from_near)
    bc_copy(2, 0, near_slot, near).wait_recv()
    bc_copy(2, 2, cross_slot, near).wait_recv()
    unfold_option(bu, 0)
    unfold_option(cu, 2)
    lax.fori_loop(pchunks, chunks, score, 0, unroll=4)

    skip = sg[...]
    skip = dot(
        jnp.concatenate(
            [
                skip.astype(jnp.bfloat16).astype(jnp.float32),
                skip - skip.astype(jnp.bfloat16).astype(jnp.float32),
                jnp.zeros((6, 8), jnp.float32),
            ],
            axis=0,
        ),
        (
            lax.broadcasted_iota(jnp.int32, (8, channels), 0)
            == lax.div(lax.broadcasted_iota(jnp.int32, (8, channels), 1), per_head)
        ).astype(jnp.float32),
    )
    skip = skip[0:1] + skip[1:2]

    loads[3].wait()

    def option_rest(at):
        def one(i, carry):
            o, k = i // ok, lax.rem(i, ok)
            p = pl.multiple_of(k * CHUNK, CHUNK)
            j = pchunks + i
            x = xpado[o, pl.ds(p + HALO, CHUNK), at].astype(jnp.float32)
            rest[i] = ee[j, :, at] * dot(scores[j], xs[j, :, at]) + skip[:, at] * x
            gates[i] = silu(go[o, pl.ds(p, CHUNK), at].astype(jnp.float32))
            return carry

        lax.fori_loop(0, opts * ok, one, 0, unroll=2)

    def output(j, lo, state, x, gate):
        at = slice(lo, lo + half)
        entering = (state * rows[j, 2:3, at]).astype(jnp.bfloat16)
        y = dot(scores[j], xs[j, :, at]) + dot(cu[j], entering)
        y = ee[j, :, at] * y + skip[:, at] * x.astype(jnp.float32)
        return y * silu(gate.astype(jnp.float32))

    pr, orr = tokens // nh, olen // nh

    def swap_copy(kind, side, to):
        packed, out = ((pack_o, got_o), (pack_p, out_p))[kind]
        return pltpu.make_async_remote_copy(
            src_ref=packed.at[side, to], dst_ref=out.at[side, h],
            send_sem=swap_send.at[kind, side], recv_sem=swap_recv.at[kind, side],
            device_id=(c, to), device_id_type=MESH,
        )

    def own_copy(kind, side):
        packed, out = ((pack_o, got_o), (pack_p, out_p))[kind]
        return pltpu.make_async_copy(packed.at[side, h], out.at[side, h], own_sem.at[kind, side])

    def send_all(kind, side):
        def send(i, carry):
            swap_copy(kind, side, partner(i)).start()
            return carry

        own_copy(kind, side).start()
        lax.fori_loop(1, nh, send, 0)

    def finish(kind, side):
        packed, out = ((pack_o, got_o), (pack_p, out_p))[kind]
        others = pl.ds(0, nh - 1)
        every = pltpu.make_async_remote_copy(
            src_ref=packed.at[side, others], dst_ref=out.at[side, others],
            send_sem=swap_send.at[kind, side], recv_sem=swap_recv.at[kind, side],
            device_id=(c, near), device_id_type=MESH,
        )
        own_copy(kind, side).wait()
        every.wait_send()
        every.wait_recv()

    for d in range(1, 4):
        dec_copy(d, lax.rem(c + 4 - d, 4)).wait_recv()
    loads[2].wait()
    for side in range(2):
        lo = side * half
        at = slice(lo, lo + half)
        option_rest(at)
        for d in range(1, 4):
            owner_copy(d, side, c, lax.rem(c + 4 - d, 4)).wait_recv()
        final = jnp.zeros((NS, half), jnp.float32)
        for i in range(4):
            final = final * dec[i, pl.ds(c, 1), at] + states[i, side, c].astype(jnp.float32)

        def option_out(o, carry, side=side, lo=lo, at=at, final=final):
            state = final
            for k in range(ok):
                j = pchunks + o * ok + k
                if k > 0:
                    grown = dot(bu[j - 1], xs[j - 1, :, at], ((0,), (0,)))
                    state = rows[j - 1, 0:1, at] * state + rows[j - 1, 1:2, at] * grown
                p = k * CHUNK
                entering = (state * rows[j, 2:3, at]).astype(jnp.bfloat16)
                y = rest[o * ok + k] + ee[j, :, at] * dot(cu[j], entering)
                m = y * gates[o * ok + k]
                some = CHUNK // orr
                ybufo[k * some : (k + 1) * some, pl.ds(pl.multiple_of(o * orr, 8), orr), :] = (
                    m.reshape(some, orr, half)
                )
            return carry

        lax.fori_loop(0, opts, option_out, 0, unroll=2)
        for i in range(nh):
            pack_o[side, i] = ybufo[i].astype(jnp.bfloat16)
        send_all(0, side)

    unfold_prefix(cu, 2)
    lax.fori_loop(0, pchunks, score, 0, unroll=4)

    for side in range(2):
        lo = side * half
        at = slice(lo, lo + half)
        for d in range(1, 4):

            @pl.when(c >= d)
            def _():
                ref = states.at[lax.rem(c + 4 - d, 4), side, pl.ds(0, 3)]
                ctx_copy(ref, st_send.at[d - 1], st_recv.at[d - 1, side], d).wait_recv()

        def prefix_out(s, carry, side=side, lo=lo, at=at):
            state = jnp.zeros((NS, half), jnp.float32)
            for i in range(3):
                step = state * dec[i, pl.ds(s, 1), at] + states[i, side, s].astype(jnp.float32)
                state = jnp.where(i < c, step, state)
            factor = jnp.ones((1, half), jnp.float32)
            for k in range(pk):
                j = s * pk + k
                now = state if k == 0 else part[s * (pk - 1) + k - 1, :, at] + state * factor
                p = k * CHUNK
                m = output(
                    j, lo, now, xpad[s, HALO + p : HALO + p + CHUNK, at], gp[s, p : p + CHUNK, at]
                )
                for n in range(half // 128):
                    ybuf[n, pl.ds(seqs * p + s, CHUNK, seqs), :] = m[:, n * 128 : (n + 1) * 128]
                factor = factor * rows[j, 0:1, at]
            return carry

        lax.fori_loop(0, seqs, prefix_out, 0, unroll=2)

        def pack(i, carry, side=side):
            start = pl.multiple_of(i * seqs * pr, 16)
            for n in range(half // 128):
                pack_p[side, i, :, n * 128 : (n + 1) * 128] = ybuf[
                    n, pl.ds(start, seqs * pr), :
                ].astype(jnp.bfloat16)
            return carry

        lax.fori_loop(0, nh, pack, 0, unroll=2)
        send_all(1, side)

    for side in range(2):
        finish(0, side)
    place = lax.broadcasted_iota(jnp.int32, (orr, 1), 0) + h * orr
    keep = [(place < length[o]).astype(jnp.float32) for o in range(opts)]
    keep = jnp.concatenate(keep, axis=0)

    def option_norm(group, carry):
        squares = None
        for i in range(4):
            for side in range(2):
                block = got_o[side, 4 * group + i].astype(jnp.float32)
                squares = block * block if squares is None else squares + block * block
        total = jnp.sum(squares, axis=1, keepdims=True)
        scale = lax.rsqrt(total / (4 * channels) + EPSILON) * keep
        for i in range(4):
            for side in range(2):
                at = pl.ds(pl.multiple_of((8 * group + 2 * i + side) * half, half), half)
                out = got_o[side, 4 * group + i].astype(jnp.float32) * scale * gain[:, at]
                res_o[:, :, at] = out.reshape(opts, orr, half).astype(jnp.bfloat16)
        return carry

    lax.fori_loop(0, nh // 4, option_norm, 0)
    option_store = pltpu.make_async_copy(res_o, out_o, load_sem.at[0])
    option_store.start()

    ctx_copy(rim.at[pl.ds(0, 3)], rim_send.at[0], rim_recv.at[0], 1).wait_send()
    ctx_copy(dec.at[pl.ds(0, 3)], dec_send.at[0], dec_recv.at[0], 1).wait_send()
    some = states.at[0, :, pl.ds(0, 3)]
    ctx_copy(some, ow_send.at[0], ow_recv.at[0, 0], 1).wait_send()
    for d in range(1, 4):

        @pl.when(c + d < 4)
        def _():
            ctx_copy(some, st_send.at[d - 1], st_recv.at[d - 1, 0], 1).wait_send()

    some = gat.at[pl.ds(0, 3)]
    pltpu.make_async_remote_copy(
        src_ref=some, dst_ref=some, send_sem=bc_send.at[0], recv_sem=bc_recv.at[0, 0],
        device_id=(c, near), device_id_type=MESH,
    ).wait_send()
    for side in range(2):
        finish(1, side)
    option_store.wait()


def norm_kernel(
    seqs, pr, values, options, gain, prefix_out, option_out,
    buf, row, res, held, sems, out_sems, rest_sems,
):
    half = values.shape[3]
    groups = values.shape[1] // 4
    width = 8 * half

    def fetch(group):
        at = pl.ds(group * 4, 4)
        return pltpu.make_async_copy(values.at[:, at], buf.at[:, at], sems.at[group])

    def store(group):
        at = pl.ds(group * width, width)
        return pltpu.make_async_copy(
            res.at[:, :, at], prefix_out.at[:, :, at], out_sems.at[group]
        )

    gain_copy = pltpu.make_async_copy(gain, row, rest_sems.at[0])
    option_in = pltpu.make_async_copy(options, held, rest_sems.at[1])
    option_copy = pltpu.make_async_copy(held, option_out, rest_sems.at[2])
    gain_copy.start()
    for group in range(groups):
        fetch(group).start()
    option_in.start()
    gain_copy.wait()
    for group in range(groups):
        fetch(group).wait()
        squares = None
        for side in range(2):
            for i in range(4):
                block = buf[side, group * 4 + i].astype(jnp.float32)
                squares = block * block if squares is None else squares + block * block
        total = jnp.sum(squares, axis=1, keepdims=True)
        scale = lax.rsqrt(total / width + EPSILON)
        for i in range(4):
            for side in range(2):
                lo = (group * 8 + i * 2 + side) * half
                at = slice(lo, lo + half)
                out = buf[side, group * 4 + i].astype(jnp.float32) * scale * row[:, at]
                res[:, :, at] = out.reshape(pr, seqs, half).astype(jnp.bfloat16)
        store(group).start()
        if group == groups // 2:
            option_in.wait()
            option_copy.start()
    for group in range(groups):
        store(group).wait()
    option_copy.wait()


def per_device(
    prefix_x,
    prefix_bc,
    prefix_gate,
    prefix_steps,
    x_kernel,
    bc_kernel,
    step_bias,
    log_rate,
    skip_gain,
    norm_gain,
    option_x,
    option_bc,
    option_gate,
    option_steps,
    option_len,
):
    nh = lax.axis_size("head")
    seqs, tokens, channels = prefix_x.shape
    opts, olen = option_x.shape[0], option_x.shape[1]
    chunks = seqs * (tokens // CHUNK) + opts * (olen // CHUNK)
    half_rows = seqs // 2 * tokens + opts // 2 * olen
    half = channels // 2
    pr, orr = tokens // nh, olen // nh
    bf16, f32 = jnp.bfloat16, jnp.float32
    anywhere = pl.BlockSpec(memory_space=pl.ANY)
    vmem = pl.BlockSpec(memory_space=pltpu.VMEM)
    dma = pltpu.SemaphoreType.DMA
    flip = functools.partial(jnp.swapaxes, axis1=1, axis2=2)

    inner = nh * channels
    gain = norm_gain.reshape(1, -1)

    swapped, normed = pl.pallas_call(
        functools.partial(mixer_kernel, nh),
        out_shape=[
            jax.ShapeDtypeStruct((2, nh, seqs * pr, half), bf16),
            jax.ShapeDtypeStruct((opts, orr, inner), bf16),
        ],
        in_specs=[anywhere, vmem, anywhere, vmem, anywhere, vmem, anywhere, vmem]
        + [vmem] * 6
        + [pl.BlockSpec(memory_space=pltpu.SMEM)],
        out_specs=[anywhere, anywhere],
        scratch_shapes=[
            pltpu.VMEM((seqs, HALO + tokens, channels), bf16),
            pltpu.VMEM((opts, HALO + olen, channels), bf16),
            pltpu.VMEM((seqs, tokens, channels), bf16),
            pltpu.VMEM((opts, olen, channels), bf16),
            pltpu.VMEM((4, HALO, channels + 128), bf16),
            pltpu.VMEM((4, half_rows, 128), bf16),
            pltpu.VMEM((4, 2, seqs, NS, half), bf16),
            pltpu.VMEM((4, 8, channels), f32),
            pltpu.VMEM((chunks, CHUNK, channels), bf16),
            pltpu.VMEM((chunks, CHUNK, channels), f32),
            pltpu.VMEM((chunks, 8, channels), f32),
            pltpu.VMEM((chunks, CHUNK, NS), bf16),
            pltpu.VMEM((chunks, CHUNK, NS), bf16),
            pltpu.VMEM((chunks, CHUNK, CHUNK), bf16),
            pltpu.VMEM((seqs * (tokens // CHUNK - 1), NS, channels), f32),
            pltpu.VMEM((half // 128, seqs * tokens, 128), f32),
            pltpu.VMEM((nh, opts * orr, half), f32),
            pltpu.VMEM((2, nh, seqs * pr, half), bf16),
            pltpu.VMEM((2, nh, opts * orr, half), bf16),
            pltpu.VMEM((opts * olen // CHUNK, CHUNK, half), f32),
            pltpu.VMEM((opts * olen // CHUNK, CHUNK, half), f32),
            pltpu.VMEM((2, 8 * chunks, 3 * CHUNK), f32),
            pltpu.VMEM((2, nh, opts * orr, half), bf16),
            pltpu.VMEM((opts, orr, inner), bf16),
            dma((4,)),
            dma((2, 2)),
            dma((1,)), dma((3,)),
            dma((1,)), dma((3, 3)),
            dma((1,)), dma((3, 2)),
            dma((3,)), dma((3, 2)),
            dma((1,)), dma((3,)),
            dma((2, 2)), dma((2, 2)),
        ],
        compiler_params=pltpu.CompilerParams(
            collective_id=0, has_side_effects=True, vmem_limit_bytes=54 * MIB
        ),
        name="mixer",
    )(
        prefix_x, flip(prefix_bc), prefix_gate, flip(prefix_steps),
        option_x, flip(option_bc), option_gate, flip(option_steps),
        x_kernel, bc_kernel,
        step_bias.reshape(1, -1), log_rate.reshape(1, -1), skip_gain.reshape(1, -1),
        gain, option_len,
    )

    prefix_out, option_out = pl.pallas_call(
        functools.partial(norm_kernel, seqs, pr),
        in_specs=[anywhere] * 3,
        out_specs=[anywhere, anywhere],
        scratch_shapes=[
            pltpu.VMEM((2, nh, seqs * pr, half), bf16),
            pltpu.VMEM((1, inner), f32),
            pltpu.VMEM((pr, seqs, inner), bf16),
            pltpu.VMEM((opts, orr, inner), bf16),
            dma((nh // 4,)),
            dma((nh // 4,)),
            dma((3,)),
        ],
        out_shape=[
            jax.ShapeDtypeStruct((pr, seqs, inner), bf16),
            jax.ShapeDtypeStruct((opts, orr, inner), bf16),
        ],
        compiler_params=pltpu.CompilerParams(vmem_limit_bytes=60 * MIB),
        name="norm",
    )(swapped, normed, gain)
    return jnp.swapaxes(prefix_out, 0, 1), option_out


def solution(mesh):
    in_specs = (
        P(None, "ctx", "head"),
        P(None, "ctx", "head"),
        P(None, "ctx", "head"),
        P(None, "ctx", "head"),
        P(None, "head"),
        P(None, "head"),
        P("head"),
        P("head"),
        P("head"),
        P(),
        P("ctx", None, "head"),
        P("ctx", None, "head"),
        P("ctx", None, "head"),
        P("ctx", None, "head"),
        P("ctx"),
    )
    out_specs = (P(None, ("ctx", "head"), None), P("ctx", "head", None))
    return jax.shard_map(
        per_device, mesh=mesh, in_specs=in_specs, out_specs=out_specs, check_vma=False
    )
```

```python
import functools

import jax
import jax.numpy as jnp
from jax import lax
from jax.experimental import pallas as pl
from jax.experimental.pallas import tpu as pltpu
from jax.sharding import PartitionSpec as P

NS = 128
GROUPS = 8
CHUNK = 128
HALO = 16
EPSILON = 1e-05
MESH = pl.DeviceIdType.MESH
MIB = 1 << 20


def silu(v):
    return v / (1.0 + jnp.exp(-v))


def dot(a, b, dims=((1,), (0,)), precision=None):
    return lax.dot_general(
        a, b, (dims, ((), ())), precision=precision, preferred_element_type=jnp.float32
    )


def conv_window(window, taps, rows):
    total = window[HALO - 3 : HALO - 3 + rows] * taps[0:1]
    for k in range(1, 4):
        total = total + window[HALO - 3 + k : HALO - 3 + k + rows] * taps[k : k + 1]
    return silu(total)


def mixer_kernel(
    heads,
    px, pbc_in, pg, pst_in, ox, obc_in, og, ost_in, xk, bck, sb, lr, sg, gain_in, length,
    out_p, out_o,
    xpad, xpado, gp, go, rim, gat, states, dec, xs, ee, rows, bu, cu, scores, part, ybuf, ybufo,
    pack_p, pack_o, rest, gates, factors, got_o, res_o, pbc, pst, obc, ost, gain,
    load_sem, own_sem, rim_send, rim_recv, bc_send, bc_recv, ow_send, ow_recv, st_send, st_recv,
    dec_send, dec_recv, swap_send, swap_recv,
):
    c = lax.axis_index("ctx")
    h = lax.axis_index("head")
    seqs, tokens, channels = px.shape
    opts, olen = ox.shape[0], ox.shape[1]
    nh = heads
    pk, ok = tokens // CHUNK, olen // CHUNK
    pchunks, chunks = seqs * pk, seqs * pk + opts * ok
    cols = pbc_in.shape[1]
    half = channels // 2
    base = (h // 4) * 4
    r = lax.rem(h, 4)
    near = base + (r + 1 - 2 * lax.rem(r, 2))
    far = base + lax.rem(r + 2, 4)
    far_slot = lax.rem(r + 2, 4)
    near_slot = near - base
    cross = base + lax.rem(near_slot + 2, 4)
    cross_slot = lax.rem(near_slot + 2, 4)
    tops = (seqs // 2 + opts // 2) * HALO
    long_p, long_o = tokens - HALO, olen - HALO
    start_o = tops + seqs // 2 * long_p
    spans = ((0, tops), (tops, seqs // 2 * long_p), (start_o, opts // 2 * long_o))

    narrow = [
        pltpu.make_async_copy(source, target, load_sem.at[4 + n])
        for n, (source, target) in enumerate(
            ((pbc_in, pbc), (obc_in, obc), (pst_in, pst), (ost_in, ost), (gain_in, gain))
        )
    ]
    for load in narrow:
        load.start()
    loads = [
        pltpu.make_async_copy(px, xpad.at[:, pl.ds(HALO, tokens), :], load_sem.at[0]),
        pltpu.make_async_copy(ox, xpado.at[:, pl.ds(HALO, olen), :], load_sem.at[1]),
        pltpu.make_async_copy(pg, gp, load_sem.at[2]),
        pltpu.make_async_copy(og, go, load_sem.at[3]),
    ]
    for load in loads:
        load.start()

    def partner(i):
        if nh != 32:
            return lax.rem(h + i, nh)
        z, y, k = h // 8, lax.rem(h // 2, 4), lax.rem(h, 2)
        dk, m = lax.rem(i, 2), i // 2
        dz, dy = lax.rem(m, 4), lax.rem(m // 4 + m, 4)
        core = lax.rem(k + dk, 2)
        return lax.rem(z + dz, 4) * 8 + lax.rem(y + dy, 4) * 2 + core

    barrier = pltpu.get_barrier_semaphore()

    def greet(i, carry):
        pl.semaphore_signal(barrier, 1, device_id=(c, lax.rem(h + i, nh)), device_id_type=MESH)
        return carry

    for d in range(1, 4):
        pl.semaphore_signal(barrier, 1, device_id=(lax.rem(c + d, 4), h), device_id_type=MESH)
    lax.fori_loop(1, nh, greet, 0)

    taps = bck[...].astype(jnp.float32)
    taps = jnp.concatenate([taps, taps], axis=1)
    blank = jnp.zeros((HALO, 2 * cols), jnp.float32)

    def pair(ref, a, count):
        both = jnp.concatenate([ref[a], ref[a + count // 2]], axis=0)
        return jnp.transpose(both.astype(jnp.float32))

    heads_p, heads_o, ends = [], [], []
    narrow[0].wait()
    for a in range(seqs // 2):
        body = pair(pbc, a, seqs)
        heads_p.append(body[0:HALO])
        ends.append(body[tokens - 3 : tokens])
        out = conv_window(body, taps, long_p)
        gat[r, tops + a * long_p : tops + (a + 1) * long_p, :] = out.astype(jnp.bfloat16)
    narrow[1].wait()
    for a in range(opts // 2):
        body = pair(obc, a, opts)
        heads_o.append(body[0:HALO])
        out = conv_window(body, taps, long_o)
        gat[r, start_o + a * long_o : start_o + (a + 1) * long_o, :] = out.astype(jnp.bfloat16)

    loads[0].wait()
    pad = jnp.zeros((HALO - 3 * seqs, channels), jnp.float32)
    tails = [xpad[s, tokens : tokens + HALO, :].astype(jnp.float32)[HALO - 3 :] for s in range(seqs)]
    rim[c, :, 0:channels] = jnp.concatenate(tails + [pad], axis=0).astype(jnp.bfloat16)
    pad = jnp.zeros((HALO - 3 * len(ends), 2 * cols), jnp.float32)
    rim[c, :, channels : channels + 2 * cols] = jnp.concatenate(ends + [pad], axis=0).astype(
        jnp.bfloat16
    )

    pl.semaphore_wait(barrier, nh + 2)

    def ctx_copy(ref, send, recv, d):
        return pltpu.make_async_remote_copy(
            src_ref=ref, dst_ref=ref, send_sem=send, recv_sem=recv,
            device_id=(lax.rem(c + d, 4), h), device_id_type=MESH,
        )

    def rim_copy(d, slot):
        return ctx_copy(rim.at[slot], rim_send.at[0], rim_recv.at[d - 1], d)

    def bc_copy(part_no, way, slot, target):
        start, count = spans[part_no]
        ref = gat.at[slot, pl.ds(start, count), :]
        return pltpu.make_async_remote_copy(
            src_ref=ref, dst_ref=ref, send_sem=bc_send.at[0],
            recv_sem=bc_recv.at[part_no, way], device_id=(c, target), device_id_type=MESH,
        )

    for d in range(1, 4):
        rim_copy(d, c).start()
    bc_copy(1, 1, r, far).start()
    bc_copy(1, 0, r, near).start()

    same = lax.broadcasted_iota(jnp.int32, (8, 8), 0) == lax.broadcasted_iota(jnp.int32, (8, 8), 1)

    def column(row):
        grown = jnp.where(same, jnp.broadcast_to(row, (8, 8)), 0.0)
        return jnp.concatenate([jnp.sum(grown, axis=1, keepdims=True)] * chunks, axis=0)

    narrow[2].wait()
    narrow[3].wait()
    raw = [pst[s, :, k * CHUNK : (k + 1) * CHUNK] for s in range(seqs) for k in range(pk)]
    raw += [ost[o, :, k * CHUNK : (k + 1) * CHUNK] for o in range(opts) for k in range(ok)]
    raw = jnp.concatenate(raw, axis=0) + column(sb[...])
    size = jnp.maximum(raw, 0.0) + jnp.log1p(jnp.exp(-jnp.abs(raw)))
    move = size * column(-jnp.exp(lr[...]))
    across = lax.broadcasted_iota(jnp.int32, (CHUNK, CHUNK), 0)
    along = lax.broadcasted_iota(jnp.int32, (CHUNK, CHUNK), 1)
    lower = across >= along
    cumul = dot(move, (across <= along).astype(jnp.float32), precision=lax.Precision.HIGHEST)
    middle, end = cumul[:, CHUNK // 2 - 1 : CHUNK // 2], cumul[:, CHUNK - 1 : CHUNK]
    place = lax.broadcasted_iota(jnp.int32, cumul.shape, 1)
    few = jnp.where(place == 0, end, jnp.where(place == 1, end - middle, middle))
    wide = [jnp.exp(middle - cumul) * size, jnp.exp(cumul - middle), jnp.exp(few)]
    for n in range(3):
        at = slice(n * CHUNK, (n + 1) * CHUNK)
        high = wide[n].astype(jnp.bfloat16).astype(jnp.float32)
        factors[0, :, at] = high
        factors[1, :, at] = wide[n] - high
    per_head = channels // 8
    pick = lax.broadcasted_iota(jnp.int32, (16, channels), 0)
    pick = lax.rem(pick, 8) == lax.div(lax.broadcasted_iota(jnp.int32, (16, channels), 1), per_head)
    pick = pick.astype(jnp.bfloat16)

    xtaps = xk[...].astype(jnp.float32)

    every = slice(0, channels)

    def convolve(j, window, cut=every):
        out = conv_window(window, xtaps[:, cut], CHUNK).astype(jnp.bfloat16)
        at = pl.multiple_of(8 * j, 8)
        both = jnp.concatenate([factors[n, pl.ds(at, 8), :] for n in range(2)], axis=0)
        grown = dot(jnp.transpose(both)[0 : 2 * CHUNK + 8].astype(jnp.bfloat16), pick[:, cut])
        xs[j, :, cut] = (out.astype(jnp.float32) * grown[0:CHUNK]).astype(jnp.bfloat16)
        ee[j, :, cut] = grown[CHUNK : 2 * CHUNK]
        rows[j, :, cut] = grown[2 * CHUNK : 2 * CHUNK + 8]
        return out

    def prefix_conv(s, k):
        at = k * CHUNK if isinstance(k, int) else pl.multiple_of(k * CHUNK, CHUNK)
        window = xpad[s, pl.ds(at, CHUNK + HALO), :].astype(jnp.float32)
        xpad[s, pl.ds(at + HALO, CHUNK), :] = convolve(s * pk + k, window)

    def option_conv(at):
        def one(i, carry):
            o, k = i // ok, ok - 1 - lax.rem(i, ok)
            p = pl.multiple_of(k * CHUNK, CHUNK)
            window = xpado[o, pl.ds(p, CHUNK + HALO), at].astype(jnp.float32)
            xpado[o, pl.ds(p + HALO, CHUNK), at] = convolve(pchunks + o * ok + k, window, at)
            return carry

        lax.fori_loop(0, opts * ok, one, 0, unroll=2)

    def later_chunks(i, carry):
        prefix_conv(i // (pk - 1), pk - 1 - lax.rem(i, pk - 1))
        return carry

    def first_chunks(s, carry):
        prefix_conv(s, 0)
        return carry

    lax.fori_loop(0, seqs * (pk - 1), later_chunks, 0, unroll=2)

    for d in range(1, 4):
        rim_copy(d, lax.rem(c + 4 - d, 4)).wait_recv()
    before = rim[lax.rem(c + 3, 4)].astype(jnp.float32) * (c > 0).astype(jnp.float32)
    last = rim[3].astype(jnp.float32)
    zeros = jnp.zeros((HALO - 3, channels), jnp.float32)
    owner_tail = jnp.zeros((3, channels), jnp.float32)
    owner_bc = jnp.zeros((3, cols), jnp.float32)
    for s in range(seqs):
        mine = (c == s).astype(jnp.float32)
        tail = before[3 * s : 3 * s + 3, 0:channels]
        xpad[s, 0:HALO, :] = jnp.concatenate([zeros, tail], axis=0).astype(jnp.bfloat16)
        owner_tail = owner_tail + last[3 * s : 3 * s + 3, 0:channels] * mine
        a, side = s % (seqs // 2), channels + cols * (s // (seqs // 2))
        owner_bc = owner_bc + last[3 * a : 3 * a + 3, side : side + cols] * mine
    loads[1].wait()
    for o in range(opts):
        xpado[o, 0:HALO, :] = jnp.concatenate([zeros, owner_tail], axis=0).astype(jnp.bfloat16)
    zeros = jnp.zeros((HALO - 3, 2 * cols), jnp.float32)
    for a in range(seqs // 2):
        tail = before[3 * a : 3 * a + 3, channels : channels + 2 * cols]
        window = jnp.concatenate([zeros, tail, heads_p[a]], axis=0)
        gat[r, a * HALO : (a + 1) * HALO, :] = conv_window(window, taps, HALO).astype(jnp.bfloat16)
    tail = jnp.concatenate([owner_bc, owner_bc], axis=1)
    for a in range(opts // 2):
        at = (seqs // 2 + a) * HALO
        window = jnp.concatenate([zeros, tail, heads_o[a]], axis=0)
        gat[r, at : at + HALO, :] = conv_window(window, taps, HALO).astype(jnp.bfloat16)
    bc_copy(0, 1, r, far).start()
    bc_copy(0, 2, r, cross).start()
    bc_copy(0, 0, r, near).start()

    def from_far():
        bc_copy(1, 1, far_slot, far).wait_recv()
        bc_copy(1, 2, far_slot, near).start()

    def from_far_side():
        bc_copy(0, 1, far_slot, far).wait_recv()
        bc_copy(0, 2, cross_slot, cross).wait_recv()
        bc_copy(1, 2, cross_slot, near).wait_recv()

    def from_near():
        bc_copy(0, 0, near_slot, near).wait_recv()
        bc_copy(1, 0, near_slot, near).wait_recv()

    has_b = r < 2
    pl.when(jnp.logical_not(has_b))(from_far)

    lax.fori_loop(0, seqs, first_chunks, 0, unroll=2)

    for s in range(seqs):
        total = rows[s * pk, 0:1, :]
        for k in range(1, pk):
            total = total * rows[s * pk + k, 0:1, :]
        dec[c, s : s + 1, :] = total

    def dec_copy(d, slot):
        return ctx_copy(dec.at[slot], dec_send.at[0], dec_recv.at[d - 1], d)

    for d in range(1, 4):
        dec_copy(d, c).start()

    left = lax.broadcasted_iota(jnp.int32, (CHUNK, 128), 1) < 64

    def unfold(to, first, top, start, low, high):
        if top is None:
            parts = [gat[first + i, pl.ds(start, CHUNK), :].astype(jnp.float32) for i in range(2)]
        else:
            parts = [
                jnp.concatenate(
                    [
                        gat[first + i, pl.ds(top, HALO), :],
                        gat[first + i, pl.ds(start, CHUNK - HALO), :],
                    ],
                    axis=0,
                ).astype(jnp.float32)
                for i in range(2)
            ]
        turned = [pltpu.roll(p, 64, 1) for p in parts]
        to[low] = jnp.where(left, parts[0], turned[1]).astype(jnp.bfloat16)
        to[high] = jnp.where(left, turned[0], parts[1]).astype(jnp.bfloat16)

    def unfold_prefix(to, first):
        def one(a, carry):
            for k in range(pk):
                top = None if k else pl.multiple_of(a * HALO, HALO)
                start = tops + a * long_p + max(k * CHUNK - HALO, 0)
                start = pl.multiple_of(start, HALO)
                unfold(to, first, top, start, a * pk + k, (a + seqs // 2) * pk + k)
            return carry

        lax.fori_loop(0, seqs // 2, one, 0)

    def unfold_option(to, first):
        def one(a, carry):
            for k in range(ok):
                top = None if k else pl.multiple_of((seqs // 2 + a) * HALO, HALO)
                start = start_o + a * long_o + max(k * CHUNK - HALO, 0)
                start = pl.multiple_of(start, HALO)
                low = pchunks + a * ok + k
                unfold(to, first, top, start, low, low + opts // 2 * ok)
            return carry

        lax.fori_loop(0, opts // 2, one, 0)

    def score(j, carry):
        raw_scores = dot(cu[j], bu[j], ((1,), (1,)))
        scores[j] = jnp.where(lower, raw_scores, 0.0).astype(jnp.bfloat16)
        return carry

    pl.when(has_b)(from_near)
    pl.when(jnp.logical_not(has_b))(from_far_side)
    unfold_prefix(bu, 0)
    bc_copy(2, 1, r, far).start()
    bc_copy(2, 0, r, near).start()

    def owner_copy(d, side, s, slot):
        return ctx_copy(
            states.at[slot, side, s], ow_send.at[0], ow_recv.at[d - 1, side], d
        )

    for d in range(1, 5):
        s = lax.rem(c + d, 4)
        state = jnp.zeros((NS, channels), jnp.float32)
        for k in range(pk):
            j = s * pk + k
            if k > 0:
                part[s * (pk - 1) + k - 1] = state
            grown = dot(bu[j], xs[j], ((0,), (0,)))
            state = rows[j, 0:1, :] * state + rows[j, 1:2, :] * grown
        for side in range(2):
            states[c, side, s] = state[:, side * half : (side + 1) * half].astype(jnp.bfloat16)
        if d < 4:
            owner_copy(d, 0, s, c).start()
    for d in range(1, 4):
        owner_copy(d, 1, lax.rem(c + d, 4), c).start()

    pl.when(has_b)(from_far)
    for side in range(2):
        for later in range(1, 4):

            @pl.when(c < later)
            def _():
                d = later - c
                for first, end_ in ((0, later), (later + 1, 4)):
                    if first < end_:
                        ref = states.at[c, side, pl.ds(first, end_ - first)]
                        ctx_copy(ref, st_send.at[d - 1], st_recv.at[d - 1, side], d).start()

    @pl.when(c > 0)
    def _():
        option_conv(slice(0, half))

    pl.when(has_b)(from_far_side)
    pl.when(jnp.logical_not(has_b))(from_near)

    skip = sg[...]
    skip = dot(
        jnp.concatenate(
            [
                skip.astype(jnp.bfloat16).astype(jnp.float32),
                skip - skip.astype(jnp.bfloat16).astype(jnp.float32),
                jnp.zeros((6, 8), jnp.float32),
            ],
            axis=0,
        ),
        (
            lax.broadcasted_iota(jnp.int32, (8, channels), 0)
            == lax.div(lax.broadcasted_iota(jnp.int32, (8, channels), 1), per_head)
        ).astype(jnp.float32),
    )
    skip = skip[0:1] + skip[1:2]

    loads[2].wait()
    loads[3].wait()

    def option_rest(at):
        def one(i, carry):
            o, k = i // ok, lax.rem(i, ok)
            p = pl.multiple_of(k * CHUNK, CHUNK)
            j = pchunks + i
            x = xpado[o, pl.ds(p + HALO, CHUNK), at].astype(jnp.float32)
            rest[i] = ee[j, :, at] * dot(scores[j], xs[j, :, at]) + skip[:, at] * x
            gates[i] = silu(go[o, pl.ds(p, CHUNK), at].astype(jnp.float32))
            return carry

        lax.fori_loop(0, opts * ok, one, 0, unroll=2)

    def output(j, lo, state, x, gate):
        at = slice(lo, lo + half)
        entering = (state * rows[j, 2:3, at]).astype(jnp.bfloat16)
        y = dot(scores[j], xs[j, :, at]) + dot(cu[j], entering)
        y = ee[j, :, at] * y + skip[:, at] * x.astype(jnp.float32)
        return y * silu(gate.astype(jnp.float32))

    pr, orr = tokens // nh, olen // nh

    def swap_copy(kind, side, to):
        packed, out = ((pack_o, got_o), (pack_p, out_p))[kind]
        return pltpu.make_async_remote_copy(
            src_ref=packed.at[side, to], dst_ref=out.at[side, h],
            send_sem=swap_send.at[kind, side], recv_sem=swap_recv.at[kind, side],
            device_id=(c, to), device_id_type=MESH,
        )

    def own_copy(kind, side):
        packed, out = ((pack_o, got_o), (pack_p, out_p))[kind]
        return pltpu.make_async_copy(packed.at[side, h], out.at[side, h], own_sem.at[kind, side])

    def send_all(kind, side):
        def fill(to):
            if kind == 0:
                pack_o[side, to] = ybufo[to].astype(jnp.bfloat16)
                return
            start = pl.multiple_of(to * seqs * pr, 16)
            for n in range(half // 128):
                pack_p[side, to, :, n * 128 : (n + 1) * 128] = ybuf[
                    n, pl.ds(start, seqs * pr), :
                ].astype(jnp.bfloat16)

        def send(i, carry):
            to = partner(i)
            fill(to)
            swap_copy(kind, side, to).start()
            return carry

        lax.fori_loop(1, nh, send, 0)
        fill(h)
        own_copy(kind, side).start()

    def finish(kind, side):
        packed, out = ((pack_o, got_o), (pack_p, out_p))[kind]
        others = pl.ds(0, nh - 1)
        every = pltpu.make_async_remote_copy(
            src_ref=packed.at[side, others], dst_ref=out.at[side, others],
            send_sem=swap_send.at[kind, side], recv_sem=swap_recv.at[kind, side],
            device_id=(c, near), device_id_type=MESH,
        )
        own_copy(kind, side).wait()
        every.wait_send()
        every.wait_recv()

    def prompts(alone):
        unfold_prefix(cu, 2)
        lax.fori_loop(0, pchunks, score, 0, unroll=4)

        for side in range(2):
            lo = side * half
            at = slice(lo, lo + half)
            for d in range(1, 1 if alone else 4):

                @pl.when(c >= d)
                def _():
                    ref = states.at[lax.rem(c + 4 - d, 4), side, pl.ds(0, 3)]
                    ctx_copy(ref, st_send.at[d - 1], st_recv.at[d - 1, side], d).wait_recv()

            def prefix_out(s, carry, side=side, lo=lo, at=at):
                state = jnp.zeros((NS, half), jnp.float32)
                for i in range(0 if alone else 3):
                    step = state * dec[i, pl.ds(s, 1), at] + states[i, side, s].astype(jnp.float32)
                    state = jnp.where(i < c, step, state)
                factor = jnp.ones((1, half), jnp.float32)
                for k in range(pk):
                    j = s * pk + k
                    now = state if k == 0 else part[s * (pk - 1) + k - 1, :, at] + state * factor
                    p = k * CHUNK
                    m = output(
                        j, lo, now, xpad[s, HALO + p : HALO + p + CHUNK, at], gp[s, p : p + CHUNK, at]
                    )
                    for n in range(half // 128):
                        ybuf[n, pl.ds(seqs * p + s, CHUNK, seqs), :] = m[:, n * 128 : (n + 1) * 128]
                    factor = factor * rows[j, 0:1, at]
                return carry

            lax.fori_loop(0, seqs, prefix_out, 0, unroll=2)

            send_all(1, side)

    @pl.when(c == 0)
    def _():
        prompts(True)
        option_conv(slice(0, half))

    bc_copy(2, 1, far_slot, far).wait_recv()
    bc_copy(2, 2, far_slot, near).start()
    bc_copy(2, 0, near_slot, near).wait_recv()
    bc_copy(2, 2, cross_slot, near).wait_recv()
    unfold_option(bu, 0)
    unfold_option(cu, 2)
    lax.fori_loop(pchunks, chunks, score, 0, unroll=4)

    for d in range(1, 4):
        dec_copy(d, lax.rem(c + 4 - d, 4)).wait_recv()
    for side in range(2):
        lo = side * half
        at = slice(lo, lo + half)
        if side == 1:
            option_conv(at)
        option_rest(at)
        for d in range(1, 4):
            owner_copy(d, side, c, lax.rem(c + 4 - d, 4)).wait_recv()
        final = jnp.zeros((NS, half), jnp.float32)
        for i in range(4):
            final = final * dec[i, pl.ds(c, 1), at] + states[i, side, c].astype(jnp.float32)

        def option_out(o, carry, side=side, lo=lo, at=at, final=final):
            state = final
            for k in range(ok):
                j = pchunks + o * ok + k
                if k > 0:
                    grown = dot(bu[j - 1], xs[j - 1, :, at], ((0,), (0,)))
                    state = rows[j - 1, 0:1, at] * state + rows[j - 1, 1:2, at] * grown
                p = k * CHUNK
                entering = (state * rows[j, 2:3, at]).astype(jnp.bfloat16)
                y = rest[o * ok + k] + ee[j, :, at] * dot(cu[j], entering)
                m = y * gates[o * ok + k]
                some = CHUNK // orr
                ybufo[k * some : (k + 1) * some, pl.ds(pl.multiple_of(o * orr, 8), orr), :] = (
                    m.reshape(some, orr, half)
                )
            return carry

        lax.fori_loop(0, opts, option_out, 0, unroll=2)
        send_all(0, side)

    pl.when(c > 0)(functools.partial(prompts, False))

    narrow[4].wait()
    for side in range(2):
        finish(0, side)
    place = lax.broadcasted_iota(jnp.int32, (orr, 1), 0) + h * orr
    keep = [(place < length[o]).astype(jnp.float32) for o in range(opts)]
    keep = jnp.concatenate(keep, axis=0)

    def option_norm(group, carry):
        squares = None
        for i in range(4):
            for side in range(2):
                block = got_o[side, 4 * group + i].astype(jnp.float32)
                squares = block * block if squares is None else squares + block * block
        total = jnp.sum(squares, axis=1, keepdims=True)
        scale = lax.rsqrt(total / (4 * channels) + EPSILON) * keep
        for i in range(4):
            for side in range(2):
                at = pl.ds(pl.multiple_of((8 * group + 2 * i + side) * half, half), half)
                out = got_o[side, 4 * group + i].astype(jnp.float32) * scale * gain[:, at]
                res_o[:, :, at] = out.reshape(opts, orr, half).astype(jnp.bfloat16)
        return carry

    lax.fori_loop(0, nh // 4, option_norm, 0)
    option_store = pltpu.make_async_copy(res_o, out_o, load_sem.at[0])
    option_store.start()

    ctx_copy(rim.at[pl.ds(0, 3)], rim_send.at[0], rim_recv.at[0], 1).wait_send()
    ctx_copy(dec.at[pl.ds(0, 3)], dec_send.at[0], dec_recv.at[0], 1).wait_send()
    some = states.at[0, :, pl.ds(0, 3)]
    ctx_copy(some, ow_send.at[0], ow_recv.at[0, 0], 1).wait_send()
    for d in range(1, 4):

        @pl.when(c + d < 4)
        def _():
            ctx_copy(some, st_send.at[d - 1], st_recv.at[d - 1, 0], 1).wait_send()

    some = gat.at[pl.ds(0, 3)]
    pltpu.make_async_remote_copy(
        src_ref=some, dst_ref=some, send_sem=bc_send.at[0], recv_sem=bc_recv.at[0, 0],
        device_id=(c, near), device_id_type=MESH,
    ).wait_send()
    for side in range(2):
        finish(1, side)
    option_store.wait()


def norm_kernel(
    seqs, pr, values, options, gain, prefix_out, option_out,
    buf, row, res, held, sems, out_sems, rest_sems,
):
    half = values.shape[3]
    groups = values.shape[1] // 4
    width = 8 * half

    def fetch(group):
        at = pl.ds(group * 4, 4)
        return pltpu.make_async_copy(values.at[:, at], buf.at[:, at], sems.at[group])

    def store(group):
        at = pl.ds(group * width, width)
        return pltpu.make_async_copy(
            res.at[:, :, at], prefix_out.at[:, :, at], out_sems.at[group]
        )

    gain_copy = pltpu.make_async_copy(gain, row, rest_sems.at[0])
    option_in = pltpu.make_async_copy(options, held, rest_sems.at[1])
    option_copy = pltpu.make_async_copy(held, option_out, rest_sems.at[2])
    gain_copy.start()
    for group in range(groups):
        fetch(group).start()
    option_in.start()
    gain_copy.wait()
    for group in range(groups):
        fetch(group).wait()
        squares = None
        for side in range(2):
            for i in range(4):
                block = buf[side, group * 4 + i].astype(jnp.float32)
                squares = block * block if squares is None else squares + block * block
        total = jnp.sum(squares, axis=1, keepdims=True)
        scale = lax.rsqrt(total / width + EPSILON)
        for i in range(4):
            for side in range(2):
                lo = (group * 8 + i * 2 + side) * half
                at = slice(lo, lo + half)
                out = buf[side, group * 4 + i].astype(jnp.float32) * scale * row[:, at]
                res[:, :, at] = out.reshape(pr, seqs, half).astype(jnp.bfloat16)
        store(group).start()
        if group == groups // 2:
            option_in.wait()
            option_copy.start()
    for group in range(groups):
        store(group).wait()
    option_copy.wait()


def per_device(
    prefix_x,
    prefix_bc,
    prefix_gate,
    prefix_steps,
    x_kernel,
    bc_kernel,
    step_bias,
    log_rate,
    skip_gain,
    norm_gain,
    option_x,
    option_bc,
    option_gate,
    option_steps,
    option_len,
):
    nh = lax.axis_size("head")
    seqs, tokens, channels = prefix_x.shape
    opts, olen = option_x.shape[0], option_x.shape[1]
    chunks = seqs * (tokens // CHUNK) + opts * (olen // CHUNK)
    half_rows = seqs // 2 * tokens + opts // 2 * olen
    half = channels // 2
    pr, orr = tokens // nh, olen // nh
    bf16, f32 = jnp.bfloat16, jnp.float32
    anywhere = pl.BlockSpec(memory_space=pl.ANY)
    vmem = pl.BlockSpec(memory_space=pltpu.VMEM)
    dma = pltpu.SemaphoreType.DMA
    flip = functools.partial(jnp.swapaxes, axis1=1, axis2=2)

    inner = nh * channels
    gain = norm_gain.reshape(1, -1)

    swapped, normed = pl.pallas_call(
        functools.partial(mixer_kernel, nh),
        out_shape=[
            jax.ShapeDtypeStruct((2, nh, seqs * pr, half), bf16),
            jax.ShapeDtypeStruct((opts, orr, inner), bf16),
        ],
        in_specs=[anywhere] * 8
        + [vmem] * 5
        + [anywhere]
        + [pl.BlockSpec(memory_space=pltpu.SMEM)],
        out_specs=[anywhere, anywhere],
        scratch_shapes=[
            pltpu.VMEM((seqs, HALO + tokens, channels), bf16),
            pltpu.VMEM((opts, HALO + olen, channels), bf16),
            pltpu.VMEM((seqs, tokens, channels), bf16),
            pltpu.VMEM((opts, olen, channels), bf16),
            pltpu.VMEM((4, HALO, channels + 128), bf16),
            pltpu.VMEM((4, half_rows, 128), bf16),
            pltpu.VMEM((4, 2, seqs, NS, half), bf16),
            pltpu.VMEM((4, 8, channels), f32),
            pltpu.VMEM((chunks, CHUNK, channels), bf16),
            pltpu.VMEM((chunks, CHUNK, channels), f32),
            pltpu.VMEM((chunks, 8, channels), f32),
            pltpu.VMEM((chunks, CHUNK, NS), bf16),
            pltpu.VMEM((chunks, CHUNK, NS), bf16),
            pltpu.VMEM((chunks, CHUNK, CHUNK), bf16),
            pltpu.VMEM((seqs * (tokens // CHUNK - 1), NS, channels), f32),
            pltpu.VMEM((half // 128, seqs * tokens, 128), f32),
            pltpu.VMEM((nh, opts * orr, half), f32),
            pltpu.VMEM((2, nh, seqs * pr, half), bf16),
            pltpu.VMEM((2, nh, opts * orr, half), bf16),
            pltpu.VMEM((opts * olen // CHUNK, CHUNK, half), f32),
            pltpu.VMEM((opts * olen // CHUNK, CHUNK, half), f32),
            pltpu.VMEM((2, 8 * chunks, 3 * CHUNK), f32),
            pltpu.VMEM((2, nh, opts * orr, half), bf16),
            pltpu.VMEM((opts, orr, inner), bf16),
            pltpu.VMEM((seqs, prefix_bc.shape[2], tokens), bf16),
            pltpu.VMEM((seqs, prefix_steps.shape[2], tokens), f32),
            pltpu.VMEM((opts, option_bc.shape[2], olen), bf16),
            pltpu.VMEM((opts, option_steps.shape[2], olen), f32),
            pltpu.VMEM((1, inner), f32),
            dma((9,)),
            dma((2, 2)),
            dma((1,)), dma((3,)),
            dma((1,)), dma((3, 3)),
            dma((1,)), dma((3, 2)),
            dma((3,)), dma((3, 2)),
            dma((1,)), dma((3,)),
            dma((2, 2)), dma((2, 2)),
        ],
        compiler_params=pltpu.CompilerParams(
            collective_id=0, has_side_effects=True, vmem_limit_bytes=54 * MIB
        ),
        name="mixer",
    )(
        prefix_x, flip(prefix_bc), prefix_gate, flip(prefix_steps),
        option_x, flip(option_bc), option_gate, flip(option_steps),
        x_kernel, bc_kernel,
        step_bias.reshape(1, -1), log_rate.reshape(1, -1), skip_gain.reshape(1, -1),
        gain, option_len,
    )

    prefix_out, option_out = pl.pallas_call(
        functools.partial(norm_kernel, seqs, pr),
        in_specs=[anywhere] * 3,
        out_specs=[anywhere, anywhere],
        scratch_shapes=[
            pltpu.VMEM((2, nh, seqs * pr, half), bf16),
            pltpu.VMEM((1, inner), f32),
            pltpu.VMEM((pr, seqs, inner), bf16),
            pltpu.VMEM((opts, orr, inner), bf16),
            dma((nh // 4,)),
            dma((nh // 4,)),
            dma((3,)),
        ],
        out_shape=[
            jax.ShapeDtypeStruct((pr, seqs, inner), bf16),
            jax.ShapeDtypeStruct((opts, orr, inner), bf16),
        ],
        compiler_params=pltpu.CompilerParams(vmem_limit_bytes=60 * MIB),
        name="norm",
    )(swapped, normed, gain)
    return jnp.swapaxes(prefix_out, 0, 1), option_out


def solution(mesh):
    in_specs = (
        P(None, "ctx", "head"),
        P(None, "ctx", "head"),
        P(None, "ctx", "head"),
        P(None, "ctx", "head"),
        P(None, "head"),
        P(None, "head"),
        P("head"),
        P("head"),
        P("head"),
        P(),
        P("ctx", None, "head"),
        P("ctx", None, "head"),
        P("ctx", None, "head"),
        P("ctx", None, "head"),
        P("ctx"),
    )
    out_specs = (P(None, ("ctx", "head"), None), P("ctx", "head", None))
    return jax.shard_map(
        per_device, mesh=mesh, in_specs=in_specs, out_specs=out_specs, check_vma=False
    )
```
